512 devices in a mesh: rep: 64 (over y, z_lo, core), fsdp: 8 (over x, z_hi).
Axes of the slice: x: 4, y: 8, z: 8 (z_hi: 2, z_lo: 4; z = z_hi * 4 + z_lo), core: 2. Of those that a mesh axis runs over, the one named last changes fastest.
Arguments:
- local_params: bfloat16 [64, 32, 14336], P('rep', 'fsdp'), may hold values from -1810 to 1810
- base: float32 [32, 14336], P('fsdp'), may hold values from -6 to 6
- momentum: float32 [32, 14336], P('fsdp'), may hold values from -4 to 4
Outputs:
- new_base: float32 [32, 14336], P('fsdp')
- new_momentum: float32 [32, 14336], P('fsdp')
The draws below stay inside these ranges and needn't reach their ends.
All inputs are finite; a program needn't handle non-finite values.
Results may differ from the reference program's by a relative error of at most 0.006.
Values may be sent and summed in bfloat16 or wider, within the bound.
No kernel may reach another device: no remote copies, remote signals or barrier semaphores. Data moves between devices by JAX's collectives and lax.ppermute only.
A program may use at most 64 MiB of HBM per device.

```python
import math
import jax
import jax.numpy as jnp
from jax import lax

FF = 14336
ROWS_DEV = 4
QBLOCK = 32
NROWS = 32
N_REP = 64


def shared_base(key):
    return jnp.clip(jax.random.normal(jax.random.fold_in(key, 11), (NROWS, FF), jnp.float32), -6.0, 6.0)


def draw_base(key, part):
    return shared_base(key)


def draw_local_params(key, part):
    anchor = shared_base(key)
    key = jax.random.fold_in(key, 2)
    keys = jax.random.split(key, 4)
    row_scale = jnp.exp(math.log(10.0) * jax.random.uniform(keys[0], (NROWS, 1), jnp.float32))
    col_scale = jnp.exp(math.log(10.0) * jax.random.uniform(keys[1], (1, FF), jnp.float32))
    rows = jnp.arange(NROWS, dtype=jnp.float32)[:, None]
    cols = jnp.arange(FF, dtype=jnp.float32)[None, :]
    inside = (jnp.mod(rows, ROWS_DEV) * FF + cols) / (ROWS_DEV * FF)
    rise = jnp.exp(math.log(3.0) * inside) * jnp.exp(math.log(3.0) * rows / NROWS)
    common = jnp.clip(jax.random.normal(keys[2], (NROWS, FF), jnp.float32), -4.0, 4.0)
    single = 4.0 * jnp.clip(jax.random.normal(keys[3], (N_REP, NROWS, FF), jnp.float32), -4.0, 4.0)
    delta = 0.1 * (common[None] + single) * (row_scale * col_scale * rise)[None]
    return (anchor[None] - delta).astype(jnp.bfloat16)


def levels(stream_key, shape, pieces, least, largest):
    def one(dim, shards_of):
        draws = jax.random.uniform(jax.random.fold_in(jax.random.fold_in(stream_key, 6), dim), (shards_of,), jnp.float32, least / len(pieces), largest / len(pieces))
        return jnp.repeat(jnp.exp(draws), shape[dim] // shards_of).reshape((-1,) + (1,) * (len(shape) - dim - 1))

    loudness = one(*pieces[0])
    for cut in pieces[1:]:
        loudness = loudness * one(*cut)
    return loudness


def noise(key, shape, scale, reach, cuts=(), kind=jnp.bfloat16):
    factor_of = levels(key, shape, cuts, -0.22, 0.18) if cuts else 1.0
    drawn = jax.random.normal(key, shape, jnp.float32) * scale * factor_of
    return jnp.minimum(jnp.maximum(drawn, -reach), reach).astype(kind)


def setup_inputs(seed: int = 0) -> dict:
    splits = jax.random.split(jax.random.key(seed), 4)
    return {
        "local_params": draw_local_params(jax.random.fold_in(splits[3], 71), 0),
        "base": draw_base(jax.random.fold_in(splits[3], 71), 0),
        "momentum": noise(splits[2], (NROWS, FF), 0.5, 4.0, ((0, 8),), jnp.float32),
    }


eps = 1e-06
clip_ratio = 0.2
outer_rate = 0.7
decay = 0.9
two_pi = 2.0 * math.pi

def staircase(values):
    return values - jnp.sin(two_pi * values) / two_pi

def quantize(values):
    shape = values.shape
    blocks = values.reshape(shape[:-1] + (shape[-1] // QBLOCK, QBLOCK))
    top = lax.optimization_barrier(jnp.max(jnp.abs(blocks), axis=-1))
    scale = ((top + eps) / 7.0).astype(jnp.bfloat16)
    code = staircase(blocks / scale.astype(jnp.float32)[..., None]).astype(jnp.bfloat16)
    return (code.reshape(shape), scale)

def dequant(code, scale):
    shape = code.shape
    blocks = code.reshape(shape[:-1] + (shape[-1] // QBLOCK, QBLOCK)).astype(jnp.float32)
    return (blocks * scale.astype(jnp.float32)[..., None]).reshape(shape)

def reference(local_params, base, momentum):

    def accumulate(total, local):
        code, scale = quantize(base - local.astype(jnp.float32))
        return (total + dequant(code, scale), None)
    total, unused = lax.scan(accumulate, jnp.zeros(base.shape, jnp.float32), local_params)
    average = total / N_REP
    code2, scale2 = quantize(average)
    grad = dequant(code2, scale2)
    norm = jnp.sqrt(jnp.sum(grad * grad))
    limit = clip_ratio * math.sqrt(NROWS * FF)
    factor = limit / jnp.maximum(norm, limit)
    scaled = factor * grad
    new_momentum = decay * momentum + scaled
    new_base = base - outer_rate * (scaled + decay * new_momentum)
    return (new_base, new_momentum)
```

```python
import math

import jax
import jax.numpy as jnp
from jax import lax
from jax.sharding import PartitionSpec as P

QBLOCK = 32


eps = 1e-06
clip_ratio = 0.2
outer_rate = 0.7
decay = 0.9
two_pi = 2.0 * math.pi


def staircase(values):
    return values - jnp.sin(two_pi * values) / two_pi


def quantize(values):
    count, length = values.shape
    blocks = values.reshape(count, length // QBLOCK, QBLOCK)
    top = jnp.max(jnp.abs(blocks), axis=-1)
    scale = ((top + eps) / 7.0).astype(jnp.bfloat16)
    code = staircase(blocks / scale.astype(jnp.float32)[..., None]).astype(jnp.bfloat16)
    return (code.reshape(count, length), scale)


def dequant(code, scale):
    count, length = code.shape
    blocks = code.reshape(count, length // QBLOCK, QBLOCK).astype(jnp.float32)
    return (blocks * scale.astype(jnp.float32)[..., None]).reshape(count, length)


def per_device(local_params, base, momentum):
    replicas = lax.axis_size("rep")
    shards = lax.axis_size("fsdp")
    rows, width = base.shape
    delta = base - local_params[0].astype(jnp.float32)
    pieces = delta.reshape(replicas, rows * width // replicas)
    code, scale = quantize(pieces)
    got = lax.all_to_all(
        jnp.concatenate([code, scale], axis=1), "rep", split_axis=0, concat_axis=0, tiled=True
    )
    got_code, got_scale = got[:, : code.shape[1]], got[:, code.shape[1] :]
    total = jnp.sum(dequant(got_code, got_scale), axis=0, keepdims=True)
    average = total / replicas
    code2, scale2 = quantize(average)
    owned = dequant(code2, scale2)
    message = jnp.concatenate([code2, scale2], axis=1)
    spread = lax.all_to_all(
        jnp.broadcast_to(message, (replicas, message.shape[1])), "rep", split_axis=0, concat_axis=0, tiled=True
    )
    all_code, all_scale = spread[:, : code2.shape[1]], spread[:, code2.shape[1] :]
    owned = dequant(all_code, all_scale)
    part = jnp.sum(owned * owned)
    squares = jnp.sum(
        lax.all_to_all(jnp.broadcast_to(part, (shards, 1, 128)), "fsdp", split_axis=0, concat_axis=0, tiled=True)[:, 0, 0]
    )
    grad = owned.reshape(rows, width)
    limit = clip_ratio * float(rows * width * shards) ** 0.5
    factor = limit / jnp.maximum(jnp.sqrt(squares), limit)
    scaled = factor * grad
    new_momentum = decay * momentum + scaled
    new_base = base - outer_rate * (scaled + decay * new_momentum)
    return (new_base, new_momentum)


def solution(mesh):
    return jax.shard_map(
        per_device,
        mesh=mesh,
        in_specs=(P("rep", "fsdp", None), P("fsdp", None), P("fsdp", None)),
        out_specs=(P("fsdp", None), P("fsdp", None)),
        check_vma=False,
    )
```

```python
import math

import jax
import jax.numpy as jnp
from jax import lax
from jax.experimental import pallas as pl
from jax.experimental.pallas import tpu as pltpu
from jax.sharding import PartitionSpec as P

QBLOCK = 32
LANES = 128
UNIT = 8

eps = 1e-06
clip_ratio = 0.2
outer_rate = 0.7
decay = 0.9

STAIR = (6.57973575592041, -12.987854957580566, 12.20757007598877, -6.687924861907959, 2.368926763534546, -0.5121700763702393)


def staircase(values):
    near = jnp.round(values)
    rest = values - near
    square = rest * rest
    poly = jnp.full_like(square, STAIR[-1])
    for coefficient in STAIR[-2::-1]:
        poly = poly * square + coefficient
    return near + rest * square * poly


def rows_of(shape):
    return lax.broadcasted_iota(jnp.int32, shape, 0) % UNIT


def lanes_of(shape):
    return lax.broadcasted_iota(jnp.int32, shape, 1) % QBLOCK


def block_ones():
    one = lax.broadcasted_iota(jnp.int32, (LANES, LANES), 0) // QBLOCK
    two = lax.broadcasted_iota(jnp.int32, (LANES, LANES), 1) // QBLOCK
    return jnp.where(one == two, 1.0, 0.0).astype(jnp.bfloat16)


def spread(values, ones):
    return jnp.dot(values.astype(jnp.bfloat16), ones, preferred_element_type=jnp.float32)


def encode(values, ones):
    shape = values.shape
    row, lane = rows_of(shape), lanes_of(shape)
    values = jnp.where(row < UNIT - 1, values, 0.0)
    top = jnp.abs(values)
    for shift in (1, 2, 4, 8, 16):
        top = jnp.maximum(top, pltpu.roll(top, shift, 1))
    scale = jnp.where(lane == QBLOCK - 1, (top + eps) * (1.0 / 7.0), 0.0)
    scale = spread(scale, ones)
    code = staircase(values / scale)
    own = jnp.where((lane == row) & (row < UNIT - 1), scale, 0.0)
    groups = (shape[0] // UNIT, UNIT, LANES)
    line = jnp.sum(own.reshape(groups), axis=1, keepdims=True)
    line = jnp.broadcast_to(line, groups).reshape(shape)
    return jnp.where(row == UNIT - 1, line, code).astype(jnp.bfloat16)


def decode(message, ones):
    shape = message.shape
    row, lane = rows_of(shape), lanes_of(shape)
    message = message.astype(jnp.float32)
    groups = (shape[0] // UNIT, UNIT, LANES)
    line = message.reshape(groups)[:, UNIT - 1 :, :]
    line = jnp.broadcast_to(line, groups).reshape(shape)
    own = jnp.where((lane == row) & (row < UNIT - 1), line, 0.0)
    return message * spread(own, ones)


def first_kernel(local_ref, base_ref, out_ref, delta_ref):
    ones = block_ones()
    rows = base_ref.shape[0]
    chunk = UNIT * UNIT
    step = rows // UNIT
    delta_ref[:rows] = base_ref[...] - local_ref[...].astype(jnp.float32)
    for a in range(UNIT):
        pieces = [delta_ref[pl.ds(a * step + s, UNIT, stride=UNIT)] for s in range(UNIT)]
        out_ref[a * chunk : (a + 1) * chunk] = encode(jnp.concatenate(pieces, axis=0), ones)


def second_kernel(in_ref, out_ref, *, replicas):
    ones = block_ones()
    chunk = UNIT * UNIT
    total = jnp.zeros((UNIT, LANES), jnp.float32)
    for a in range(UNIT):
        values = decode(in_ref[a * chunk : (a + 1) * chunk], ones)
        total += jnp.sum(values.reshape(UNIT, UNIT, LANES), axis=0)
    message = encode(total / replicas, ones)
    message = jnp.concatenate([message.astype(jnp.float32)] * UNIT, axis=0).astype(jnp.bfloat16)
    for a in range(UNIT):
        out_ref[a * chunk : (a + 1) * chunk] = message


def third_kernel(in_ref, grad_ref, squares_ref):
    ones = block_ones()
    chunk = UNIT * UNIT
    step = grad_ref.shape[0] // UNIT
    total = jnp.zeros((UNIT, LANES), jnp.float32)
    for a in range(UNIT):
        values = decode(in_ref[a * chunk : (a + 1) * chunk], ones)
        total += jnp.sum((values * values).reshape(UNIT, UNIT, LANES), axis=0)
        for s in range(UNIT):
            grad_ref[pl.ds(a * step + s, UNIT - 1, stride=UNIT)] = values[s * UNIT : s * UNIT + UNIT - 1]
    squares_ref[...] = jnp.full((UNIT, LANES), jnp.sum(total), jnp.float32)


def fourth_kernel(grad_ref, base_ref, momentum_ref, squares_ref, new_base_ref, new_momentum_ref, *, limit):
    squares = jnp.sum(squares_ref[...], axis=0, keepdims=True)
    factor = limit / jnp.maximum(jnp.sqrt(squares), limit)
    scaled = factor * grad_ref[...]
    momentum = decay * momentum_ref[...] + scaled
    new_momentum_ref[...] = momentum
    new_base_ref[...] = base_ref[...] - outer_rate * (scaled + decay * momentum)


def to_units(array):
    rows, width = array.shape
    return array.reshape(rows, width // LANES, LANES).transpose(1, 0, 2).reshape(rows * width // LANES, LANES)


def from_units(array, rows, width):
    return array.reshape(width // LANES, rows, LANES).transpose(1, 0, 2).reshape(rows, width)


def per_device(groups, local_params, base, momentum):
    replicas = lax.axis_size("rep")
    shards = lax.axis_size("fsdp")
    rows, width = base.shape
    units = rows * width // LANES
    f32 = jnp.float32
    message = jax.ShapeDtypeStruct((replicas * UNIT, LANES), jnp.bfloat16)

    def exchange(array):
        array = array.reshape(replicas, UNIT, LANES)
        return lax.all_to_all(array, "rep", split_axis=0, concat_axis=0, tiled=True).reshape(message.shape)

    base_units = to_units(base)
    pieces = pl.pallas_call(
        first_kernel,
        out_shape=message,
        scratch_shapes=[pltpu.VMEM((units + UNIT * UNIT, LANES), f32)],
    )(to_units(local_params[0]), base_units)
    owned = pl.pallas_call(
        lambda *refs: second_kernel(*refs, replicas=replicas),
        out_shape=message,
    )(exchange(pieces))
    grad, squares = pl.pallas_call(
        third_kernel,
        out_shape=(jax.ShapeDtypeStruct((units, LANES), f32), jax.ShapeDtypeStruct((shards, LANES), f32)),
    )(exchange(owned))
    squares = lax.all_to_all(
        squares.reshape(shards, 1, LANES), ("rep", "fsdp"), split_axis=0, concat_axis=0, tiled=True, axis_index_groups=groups
    ).reshape(shards, LANES)
    limit = clip_ratio * float(rows * width * shards) ** 0.5
    new_base, new_momentum = pl.pallas_call(
        lambda *refs: fourth_kernel(*refs, limit=limit),
        out_shape=(jax.ShapeDtypeStruct((units, LANES), f32),) * 2,
    )(grad, base_units, to_units(momentum), squares)
    return from_units(new_base, rows, width), from_units(new_momentum, rows, width)


def near_groups(mesh):
    replicas, shards = mesh.shape["rep"], mesh.shape["fsdp"]

    def index(y, z, core, x):
        return ((y * 4 + z % 4) * 2 + core) * shards + x * 2 + z // 4

    partner = {0: 6, 1: 7, 2: 4, 3: 5}
    return [
        [index(y, z, core, x) for x in range(shards // 2) for z in (low, partner[low])]
        for y in range(replicas // 8)
        for low in range(4)
        for core in range(2)
    ]


def solution(mesh):
    groups = near_groups(mesh)
    return jax.shard_map(
        lambda *arrays: per_device(groups, *arrays),
        mesh=mesh,
        in_specs=(P("rep", "fsdp", None), P("fsdp", None), P("fsdp", None)),
        out_specs=(P("fsdp", None), P("fsdp", None)),
        check_vma=False,
    )
```

```python
import math

import jax
import jax.numpy as jnp
from jax import lax
from jax.experimental import pallas as pl
from jax.experimental.pallas import tpu as pltpu
from jax.sharding import PartitionSpec as P

QBLOCK = 32
LANES = 128
UNIT = 8
PARAMS = pltpu.CompilerParams(vmem_limit_bytes=4 << 20)

eps = 1e-06
clip_ratio = 0.2
outer_rate = 0.7
decay = 0.9

STAIR = (6.57973575592041, -12.987854957580566, 12.20757007598877, -6.687924861907959, 2.368926763534546, -0.5121700763702393)


def staircase(values):
    near = jnp.round(values)
    rest = values - near
    square = rest * rest
    poly = jnp.full_like(square, STAIR[-1])
    for coefficient in STAIR[-2::-1]:
        poly = poly * square + coefficient
    return near + rest * square * poly


def rows_of(shape):
    return lax.broadcasted_iota(jnp.int32, shape, 0) % UNIT


def lanes_of(shape):
    return lax.broadcasted_iota(jnp.int32, shape, 1) % QBLOCK


def block_ones():
    one = lax.broadcasted_iota(jnp.int32, (LANES, LANES), 0) // QBLOCK
    two = lax.broadcasted_iota(jnp.int32, (LANES, LANES), 1) // QBLOCK
    return jnp.where(one == two, 1.0, 0.0).astype(jnp.bfloat16)


def spread(values, ones):
    return jnp.dot(values.astype(jnp.bfloat16), ones, preferred_element_type=jnp.float32)


def encode(values, ones):
    shape = values.shape
    row, lane = rows_of(shape), lanes_of(shape)
    values = jnp.where(row < UNIT - 1, values, 0.0)
    top = jnp.abs(values)
    for shift in (1, 2, 4, 8, 16):
        top = jnp.maximum(top, pltpu.roll(top, shift, 1))
    scale = jnp.where(lane == QBLOCK - 1, (top + eps) * (1.0 / 7.0), 0.0)
    scale = spread(scale, ones)
    code = staircase(values / scale)
    own = jnp.where((lane == row) & (row < UNIT - 1), scale, 0.0)
    groups = (shape[0] // UNIT, UNIT, LANES)
    line = jnp.sum(own.reshape(groups), axis=1, keepdims=True)
    line = jnp.broadcast_to(line, groups).reshape(shape)
    return jnp.where(row == UNIT - 1, line, code).astype(jnp.bfloat16)


def decode(message, ones):
    shape = message.shape
    row, lane = rows_of(shape), lanes_of(shape)
    message = message.astype(jnp.float32)
    groups = (shape[0] // UNIT, UNIT, LANES)
    line = message.reshape(groups)[:, UNIT - 1 :, :]
    line = jnp.broadcast_to(line, groups).reshape(shape)
    own = jnp.where((lane == row) & (row < UNIT - 1), line, 0.0)
    return message * spread(own, ones)


def first_kernel(local_ref, base_ref, out_ref, delta_ref):
    ones = block_ones()
    rows = base_ref.shape[0]
    chunk = UNIT * UNIT
    step = rows // UNIT
    delta_ref[:rows] = base_ref[...] - local_ref[...].astype(jnp.float32)
    for a in range(UNIT):
        pieces = [delta_ref[pl.ds(a * step + s, UNIT, stride=UNIT)] for s in range(UNIT)]
        out_ref[a * chunk : (a + 1) * chunk] = encode(jnp.concatenate(pieces, axis=0), ones)


def second_kernel(in_ref, out_ref, *, replicas):
    ones = block_ones()
    chunk = UNIT * UNIT
    total = jnp.zeros((UNIT, LANES), jnp.float32)
    for a in range(UNIT):
        values = decode(in_ref[a * chunk : (a + 1) * chunk], ones)
        total += jnp.sum(values.reshape(UNIT, UNIT, LANES), axis=0)
    message = encode(total / replicas, ones)
    message = jnp.concatenate([message.astype(jnp.float32)] * UNIT, axis=0).astype(jnp.bfloat16)
    for a in range(UNIT):
        out_ref[a * chunk : (a + 1) * chunk] = message


def third_kernel(in_ref, grad_ref, squares_ref):
    ones = block_ones()
    chunk = UNIT * UNIT
    step = grad_ref.shape[0] // UNIT
    total = jnp.zeros((UNIT, LANES), jnp.float32)
    for a in range(UNIT):
        values = decode(in_ref[a * chunk : (a + 1) * chunk], ones)
        total += jnp.sum((values * values).reshape(UNIT, UNIT, LANES), axis=0)
        for s in range(UNIT):
            grad_ref[pl.ds(a * step + s, UNIT - 1, stride=UNIT)] = values[s * UNIT : s * UNIT + UNIT - 1]
    squares_ref[...] = jnp.full((UNIT, LANES), jnp.sum(total), jnp.float32)


def fourth_kernel(grad_ref, base_ref, momentum_ref, squares_ref, new_base_ref, new_momentum_ref, *, limit):
    squares = jnp.sum(squares_ref[...], axis=0, keepdims=True)
    factor = limit / jnp.maximum(jnp.sqrt(squares), limit)
    scaled = factor * grad_ref[...]
    momentum = decay * momentum_ref[...] + scaled
    new_momentum_ref[...] = momentum
    new_base_ref[...] = base_ref[...] - outer_rate * (scaled + decay * momentum)


def to_units(array):
    rows, width = array.shape
    return array.reshape(rows, width // LANES, LANES).transpose(1, 0, 2).reshape(rows * width // LANES, LANES)


def from_units(array, rows, width):
    return array.reshape(width // LANES, rows, LANES).transpose(1, 0, 2).reshape(rows, width)


def per_device(groups, local_params, base, momentum):
    replicas = lax.axis_size("rep")
    shards = lax.axis_size("fsdp")
    rows, width = base.shape
    units = rows * width // LANES
    f32 = jnp.float32
    message = jax.ShapeDtypeStruct((replicas * UNIT, LANES), jnp.bfloat16)

    def exchange(array):
        array = array.reshape(replicas, UNIT, LANES)
        return lax.all_to_all(array, "rep", split_axis=0, concat_axis=0, tiled=True).reshape(message.shape)

    base_units = to_units(base)
    pieces = pl.pallas_call(
        first_kernel,
        compiler_params=PARAMS,
        out_shape=message,
        scratch_shapes=[pltpu.VMEM((units + UNIT * UNIT, LANES), f32)],
    )(to_units(local_params[0]), base_units)
    owned = pl.pallas_call(
        lambda *refs: second_kernel(*refs, replicas=replicas),
        compiler_params=PARAMS,
        out_shape=message,
    )(exchange(pieces))
    grad, squares = pl.pallas_call(
        third_kernel,
        compiler_params=PARAMS,
        out_shape=(jax.ShapeDtypeStruct((units, LANES), f32), jax.ShapeDtypeStruct((shards, LANES), f32)),
    )(exchange(owned))
    squares = lax.all_to_all(
        squares.reshape(shards, 1, LANES), ("rep", "fsdp"), split_axis=0, concat_axis=0, tiled=True, axis_index_groups=groups
    ).reshape(shards, LANES)
    limit = clip_ratio * float(rows * width * shards) ** 0.5
    new_base, new_momentum = pl.pallas_call(
        lambda *refs: fourth_kernel(*refs, limit=limit),
        compiler_params=PARAMS,
        out_shape=(jax.ShapeDtypeStruct((units, LANES), f32),) * 2,
    )(grad, base_units, to_units(momentum), squares)
    return from_units(new_base, rows, width), from_units(new_momentum, rows, width)


def near_groups(mesh):
    replicas, shards = mesh.shape["rep"], mesh.shape["fsdp"]

    def index(y, z, core, x):
        return ((y * 4 + z % 4) * 2 + core) * shards + x * 2 + z // 4

    partner = {0: 6, 1: 7, 2: 4, 3: 5}
    return [
        [index(y, z, core, x) for x in range(shards // 2) for z in (low, partner[low])]
        for y in range(replicas // 8)
        for low in range(4)
        for core in range(2)
    ]


def solution(mesh):
    groups = near_groups(mesh)
    return jax.shard_map(
        lambda *arrays: per_device(groups, *arrays),
        mesh=mesh,
        in_specs=(P("rep", "fsdp", None), P("fsdp", None), P("fsdp", None)),
        out_specs=(P("fsdp", None), P("fsdp", None)),
        check_vma=False,
    )
```

```python
import math

import jax
import jax.numpy as jnp
from jax import lax
from jax.experimental import pallas as pl
from jax.experimental.pallas import tpu as pltpu
from jax.sharding import PartitionSpec as P

QBLOCK = 32
LANES = 128
UNIT = 8
PARAMS = pltpu.CompilerParams(vmem_limit_bytes=4 << 20)

eps = 1e-06
clip_ratio = 0.2
outer_rate = 0.7
decay = 0.9

STAIR = (6.57973575592041, -12.987854957580566, 12.20757007598877, -6.687924861907959, 2.368926763534546, -0.5121700763702393)


def staircase(values):
    near = jnp.round(values)
    rest = values - near
    square = rest * rest
    poly = jnp.full_like(square, STAIR[-1])
    for coefficient in STAIR[-2::-1]:
        poly = poly * square + coefficient
    return near + rest * square * poly


def rows_of(shape):
    return lax.broadcasted_iota(jnp.int32, shape, 0) % UNIT


def lanes_of(shape):
    return lax.broadcasted_iota(jnp.int32, shape, 1) % QBLOCK


def block_ones():
    one = lax.broadcasted_iota(jnp.int32, (LANES, LANES), 0) // QBLOCK
    two = lax.broadcasted_iota(jnp.int32, (LANES, LANES), 1) // QBLOCK
    return jnp.where(one == two, 1.0, 0.0).astype(jnp.bfloat16)


def spread(values, ones):
    return jnp.dot(values.astype(jnp.bfloat16), ones, preferred_element_type=jnp.float32)


def encode(values, ones):
    shape = values.shape
    row, lane = rows_of(shape), lanes_of(shape)
    values = jnp.where(row < UNIT - 1, values, 0.0)
    top = jnp.abs(values)
    for shift in (1, 2, 4, 8, 16):
        top = jnp.maximum(top, pltpu.roll(top, shift, 1))
    scale = jnp.where(lane == QBLOCK - 1, (top + eps) * (1.0 / 7.0), 0.0)
    scale = spread(scale, ones)
    code = staircase(values / scale)
    own = jnp.where((lane == row) & (row < UNIT - 1), scale, 0.0)
    groups = (shape[0] // UNIT, UNIT, LANES)
    line = jnp.sum(own.reshape(groups), axis=1, keepdims=True)
    line = jnp.broadcast_to(line, groups).reshape(shape)
    return jnp.where(row == UNIT - 1, line, code).astype(jnp.bfloat16)


def decode(message, ones):
    shape = message.shape
    row, lane = rows_of(shape), lanes_of(shape)
    message = message.astype(jnp.float32)
    groups = (shape[0] // UNIT, UNIT, LANES)
    line = message.reshape(groups)[:, UNIT - 1 :, :]
    line = jnp.broadcast_to(line, groups).reshape(shape)
    own = jnp.where((lane == row) & (row < UNIT - 1), line, 0.0)
    return message * spread(own, ones)


def first_kernel(local_ref, base_ref, out_ref, delta_ref):
    ones = block_ones()
    rows = base_ref.shape[0]
    chunk = UNIT * UNIT
    step = rows // UNIT
    delta_ref[:rows] = base_ref[...] - local_ref[...].astype(jnp.float32)
    for a in range(UNIT):
        pieces = [delta_ref[pl.ds(a * step + s, UNIT, stride=UNIT)] for s in range(UNIT)]
        out_ref[a * chunk : (a + 1) * chunk] = encode(jnp.concatenate(pieces, axis=0), ones)


def second_kernel(in_ref, out_ref, *, replicas):
    ones = block_ones()
    chunk = UNIT * UNIT
    total = jnp.zeros((UNIT, LANES), jnp.float32)
    for a in range(UNIT):
        values = decode(in_ref[a * chunk : (a + 1) * chunk], ones)
        total += jnp.sum(values.reshape(UNIT, UNIT, LANES), axis=0)
    message = encode(total / replicas, ones)
    message = jnp.concatenate([message.astype(jnp.float32)] * UNIT, axis=0).astype(jnp.bfloat16)
    for a in range(UNIT):
        out_ref[a * chunk : (a + 1) * chunk] = message


def third_kernel(in_ref, grad_ref, squares_ref):
    ones = block_ones()
    chunk = UNIT * UNIT
    step = grad_ref.shape[0] // UNIT
    total = jnp.zeros((UNIT, LANES), jnp.float32)
    for a in range(UNIT):
        values = decode(in_ref[a * chunk : (a + 1) * chunk], ones)
        total += jnp.sum((values * values).reshape(UNIT, UNIT, LANES), axis=0)
        for s in range(UNIT):
            grad_ref[pl.ds(a * step + s, UNIT - 1, stride=UNIT)] = values[s * UNIT : s * UNIT + UNIT - 1]
    squares_ref[...] = jnp.full((UNIT, LANES), jnp.sum(total), jnp.float32)


def fourth_kernel(grad_ref, base_ref, momentum_ref, squares_ref, new_base_ref, new_momentum_ref, *, limit):
    squares = jnp.sum(squares_ref[...], axis=0, keepdims=True)
    factor = limit / jnp.maximum(jnp.sqrt(squares), limit)
    scaled = factor * grad_ref[...]
    momentum = decay * momentum_ref[...] + scaled
    new_momentum_ref[...] = momentum
    new_base_ref[...] = base_ref[...] - outer_rate * (scaled + decay * momentum)


def to_units(array):
    rows, width = array.shape
    return array.reshape(rows, width // LANES, LANES).transpose(1, 0, 2).reshape(rows * width // LANES, LANES)


def from_units(array, rows, width):
    return array.reshape(width // LANES, rows, LANES).transpose(1, 0, 2).reshape(rows, width)


def per_device(groups, local_params, base, momentum):
    replicas = lax.axis_size("rep")
    shards = lax.axis_size("fsdp")
    rows, width = base.shape
    units = rows * width // LANES
    f32 = jnp.float32
    message = jax.ShapeDtypeStruct((replicas * UNIT, LANES), jnp.bfloat16)

    def exchange(array):
        array = array.reshape(replicas, UNIT, LANES)
        return lax.all_to_all(array, "rep", split_axis=0, concat_axis=0, tiled=True).reshape(message.shape)

    base_units = to_units(base)
    pieces = pl.pallas_call(
        first_kernel,
        compiler_params=PARAMS,
        out_shape=message,
        scratch_shapes=[pltpu.VMEM((units + UNIT * UNIT, LANES), f32)],
    )(to_units(local_params[0]), base_units)
    owned = pl.pallas_call(
        lambda *refs: second_kernel(*refs, replicas=replicas),
        compiler_params=PARAMS,
        out_shape=message,
    )(exchange(pieces))
    grad, squares = pl.pallas_call(
        third_kernel,
        compiler_params=PARAMS,
        out_shape=(jax.ShapeDtypeStruct((units, LANES), f32), jax.ShapeDtypeStruct((shards, LANES), f32)),
    )(exchange(owned))
    squares = lax.all_to_all(
        squares.reshape(shards, 1, LANES), ("rep", "fsdp"), split_axis=0, concat_axis=0, tiled=True, axis_index_groups=groups
    ).reshape(shards, LANES)
    limit = clip_ratio * float(rows * width * shards) ** 0.5
    new_base, new_momentum = pl.pallas_call(
        lambda *refs: fourth_kernel(*refs, limit=limit),
        compiler_params=PARAMS,
        out_shape=(jax.ShapeDtypeStruct((units, LANES), f32),) * 2,
    )(grad, base_units, to_units(momentum), squares)
    return from_units(new_base, rows, width), from_units(new_momentum, rows, width)


def near_groups(mesh):
    replicas, shards = mesh.shape["rep"], mesh.shape["fsdp"]

    def index(y, z, core, x):
        return ((y * 4 + z % 4) * 2 + core) * shards + x * 2 + z // 4

    partner = {0: 6, 1: 7, 2: 4, 3: 5}
    return [
        [index(y, z, core ^ (z // 4), x) for x in range(shards // 2) for z in (low, partner[low])]
        for y in range(replicas // 8)
        for low in range(4)
        for core in range(2)
    ]


def solution(mesh):
    groups = near_groups(mesh)
    return jax.shard_map(
        lambda *arrays: per_device(groups, *arrays),
        mesh=mesh,
        in_specs=(P("rep", "fsdp", None), P("fsdp", None), P("fsdp", None)),
        out_specs=(P("fsdp", None), P("fsdp", None)),
        check_vma=False,
    )
```

```python
import math

import jax
import jax.numpy as jnp
from jax import lax
from jax.experimental import pallas as pl
from jax.experimental.pallas import tpu as pltpu
from jax.sharding import PartitionSpec as P

QBLOCK = 32
LANES = 128
UNIT = 8
CHUNK = UNIT * UNIT
PARAMS = pltpu.CompilerParams(vmem_limit_bytes=4 << 20)

eps = 1e-06
clip_ratio = 0.2
outer_rate = 0.7
decay = 0.9

STAIR = (6.57973575592041, -12.987854957580566, 12.20757007598877, -6.687924861907959, 2.368926763534546, -0.5121700763702393)


def staircase(values):
    near = jnp.round(values)
    rest = values - near
    square = rest * rest
    poly = jnp.full_like(square, STAIR[-1])
    for coefficient in STAIR[-2::-1]:
        poly = poly * square + coefficient
    return near + rest * square * poly


def index_of(shape, axis):
    return lax.broadcasted_iota(jnp.int32, shape, axis)


def zero_one(condition):
    return jnp.where(condition, 1.0, 0.0).astype(jnp.bfloat16)


def block_ones():
    shape = (LANES, LANES)
    return zero_one(index_of(shape, 0) // QBLOCK == index_of(shape, 1) // QBLOCK)


def own_lane(shape):
    row, lane = index_of(shape, 0) % UNIT, index_of(shape, 1) % QBLOCK
    return (row == lane) & (row < UNIT - 1)


def dot(one, two):
    return jnp.dot(one.astype(jnp.bfloat16), two, preferred_element_type=jnp.float32)


def packed_top(arrays, lane):
    arrays = [jnp.abs(array) for array in arrays]
    shift = QBLOCK // 2
    while shift:
        halves = []
        for one, two in zip(arrays[::2], arrays[1::2]):
            one = jnp.maximum(one, pltpu.roll(one, shift, 1))
            two = jnp.maximum(two, pltpu.roll(two, LANES - shift, 1))
            halves.append(jnp.where(lane & shift != 0, one, two))
        arrays = halves
        shift //= 2
    return arrays[0]


def place_of(j):
    return sum((QBLOCK // 2) >> bit for bit in range(5) if not (j >> bit) & 1)


def swap(values, lane, shift):
    return jnp.where(lane & shift == 0, pltpu.roll(values, LANES - shift, 1), pltpu.roll(values, shift, 1))


def full_top(values, lane):
    top = jnp.abs(values)
    for shift in (1, 4):
        down = [pltpu.roll(top, LANES - shift * k, 1) for k in (1, 2, 3)]
        up = [pltpu.roll(top, shift * k, 1) for k in (1, 2, 3)]
        place = (lane // shift) % 4
        first = jnp.where(place < 3, down[0], up[0])
        second = jnp.where(place < 2, down[1], up[1])
        third = jnp.where(place == 0, down[2], jnp.where(place == 3, up[2], up[0]))
        top = jnp.maximum(jnp.maximum(top, first), jnp.maximum(second, third))
    return jnp.maximum(top, swap(top, lane, 16))


def scale_of(top):
    return ((top + eps) * (1.0 / 7.0)).astype(jnp.bfloat16).astype(jnp.float32)


def encode(values):
    shape = values.shape
    row, lane = index_of(shape, 0), index_of(shape, 1) % QBLOCK
    scale = scale_of(full_top(values, lane))
    code = staircase(values * pl.reciprocal(scale))
    line = jnp.sum(jnp.where(own_lane(shape), scale, 0.0), axis=0, keepdims=True)
    return jnp.where(row == UNIT - 1, line, code)


def decode(message, ones):
    shape = message.shape
    message = message.astype(jnp.float32)
    groups = (shape[0] // UNIT, UNIT, LANES)
    line = message.reshape(groups)[:, UNIT - 1 :, :]
    line = jnp.broadcast_to(line, groups).reshape(shape)
    return message * dot(jnp.where(own_lane(shape), line, 0.0), ones)


def first_kernel(local_ref, base_ref, out_ref, local_buffer, base_buffer, delta_ref, scale_ref, code_ref, sems):
    rows = base_ref.shape[0]
    step = rows // UNIT
    copies = [
        pltpu.make_async_copy(base_ref, base_buffer, sems.at[0]),
        pltpu.make_async_copy(local_ref, local_buffer, sems.at[1]),
    ]
    for copy in copies:
        copy.start()
    ones = block_ones()
    lane = index_of((UNIT, LANES), 1) % QBLOCK
    for copy in copies:
        copy.wait()
    delta_ref[:rows] = base_buffer[...] - local_buffer[...].astype(jnp.float32)
    pieces = [delta_ref[pl.ds(a * step + s, UNIT, stride=UNIT)] for a in range(UNIT) for s in range(UNIT)]
    scales = []
    for first in range(0, len(pieces), QBLOCK):
        scale = scale_of(packed_top(pieces[first : first + QBLOCK], lane))
        scales += [jnp.where(lane == place_of(j), scale, 0.0) for j in range(QBLOCK)]
    for a in range(UNIT):
        here = pl.ds(a * CHUNK, CHUNK)
        group = slice(a * UNIT, (a + 1) * UNIT)
        scale = dot(jnp.concatenate(scales[group], axis=0), ones)
        scale_ref[here] = scale
        code_ref[here] = staircase(jnp.concatenate(pieces[group], axis=0) * pl.reciprocal(scale))
        line = jnp.zeros((UNIT, LANES), jnp.float32)
        for s in range(UNIT - 1):
            line = jnp.where(lane == s, scale_ref[pl.ds(a * CHUNK + s, UNIT, stride=UNIT)], line)
        code_ref[pl.ds(a * CHUNK + UNIT - 1, UNIT, stride=UNIT)] = line
        out_ref[here] = code_ref[here].astype(jnp.bfloat16)


def second_kernel(in_ref, out_ref, *, replicas):
    ones = block_ones()
    total = jnp.zeros((UNIT, LANES), jnp.float32)
    values = decode(in_ref[...], ones)
    total += jnp.sum(values.reshape(CHUNK, UNIT, LANES), axis=0)
    message = jnp.concatenate([encode(total / replicas)] * UNIT, axis=0).astype(jnp.bfloat16)
    for a in range(UNIT):
        out_ref[a * CHUNK : (a + 1) * CHUNK] = message


def third_kernel(in_ref, grad_ref, squares_ref):
    ones = block_ones()
    step = grad_ref.shape[0] // UNIT
    total = jnp.zeros((UNIT, LANES), jnp.float32)
    values = decode(in_ref[...], ones)
    total += jnp.sum((values * values).reshape(CHUNK, UNIT, LANES), axis=0)
    for a in range(UNIT):
        for s in range(UNIT):
            first = (a * UNIT + s) * UNIT
            grad_ref[pl.ds(a * step + s, UNIT - 1, stride=UNIT)] = values[first : first + UNIT - 1]
    squares_ref[...] = jnp.full((UNIT, LANES), jnp.sum(total), jnp.float32)


def fourth_kernel(grad_ref, base_ref, momentum_ref, squares_ref, new_base_ref, new_momentum_ref, *, limit):
    squares = jnp.sum(squares_ref[...], axis=0, keepdims=True)
    factor = limit / jnp.maximum(jnp.sqrt(squares), limit)
    scaled = factor * grad_ref[...]
    momentum = decay * momentum_ref[...] + scaled
    new_momentum_ref[...] = momentum
    new_base_ref[...] = base_ref[...] - outer_rate * (scaled + decay * momentum)


def to_units(array):
    rows, width = array.shape
    return array.reshape(rows, width // LANES, LANES).transpose(1, 0, 2).reshape(rows * width // LANES, LANES)


def from_units(array, rows, width):
    return array.reshape(width // LANES, rows, LANES).transpose(1, 0, 2).reshape(rows, width)


def run_first(local_units, base_units):
    units = base_units.shape[0]
    return pl.pallas_call(
        first_kernel, name="encode_pieces",
        compiler_params=PARAMS,
        in_specs=[pl.BlockSpec(memory_space=pltpu.HBM)] * 2,
        out_shape=jax.ShapeDtypeStruct((CHUNK * UNIT, LANES), jnp.bfloat16),
        scratch_shapes=[
            pltpu.VMEM((units, LANES), jnp.bfloat16),
            pltpu.VMEM((units, LANES), jnp.float32),
            pltpu.VMEM((units + CHUNK, LANES), jnp.float32),
            pltpu.VMEM((CHUNK * UNIT, LANES), jnp.float32),
            pltpu.VMEM((CHUNK * UNIT, LANES), jnp.float32),
            pltpu.SemaphoreType.DMA((2,)),
        ],
    )(*(pltpu.with_memory_space_constraint(array, pltpu.HBM) for array in (local_units, base_units)))


def run_second(message, replicas):
    return pl.pallas_call(
        lambda *refs: second_kernel(*refs, replicas=replicas),name="add_and_encode",
        compiler_params=PARAMS,
        out_shape=jax.ShapeDtypeStruct((CHUNK * UNIT, LANES), jnp.bfloat16),
    )(message)


def run_third(message, units):
    return pl.pallas_call(
        third_kernel, name="decode_all",
        compiler_params=PARAMS,
        out_shape=(jax.ShapeDtypeStruct((units, LANES), jnp.float32), jax.ShapeDtypeStruct((UNIT, LANES), jnp.float32)),
    )(message)


def run_fourth(grad, base_units, momentum_units, squares, limit):
    units = base_units.shape[0]
    return pl.pallas_call(
        lambda *refs: fourth_kernel(*refs, limit=limit),
        compiler_params=PARAMS,
        name="update",
        out_shape=(jax.ShapeDtypeStruct((units, LANES), jnp.float32),) * 2,
    )(grad, base_units, momentum_units, squares)


def per_device(groups, local_params, base, momentum):
    replicas = lax.axis_size("rep")
    shards = lax.axis_size("fsdp")
    rows, width = base.shape

    def exchange(array):
        array = array.reshape(replicas, UNIT, LANES)
        return lax.all_to_all(array, "rep", split_axis=0, concat_axis=0, tiled=True).reshape(replicas * UNIT, LANES)

    base_units = to_units(base)
    pieces = run_first(to_units(local_params[0]), base_units)
    owned = run_second(exchange(pieces), replicas)
    grad, squares = run_third(exchange(owned), base_units.shape[0])
    squares = lax.all_to_all(
        squares.reshape(shards, 1, LANES), ("rep", "fsdp"), split_axis=0, concat_axis=0, tiled=True, axis_index_groups=groups
    ).reshape(shards, LANES)
    limit = clip_ratio * float(rows * width * shards) ** 0.5
    new_base, new_momentum = run_fourth(grad, base_units, to_units(momentum), squares, limit)
    return from_units(new_base, rows, width), from_units(new_momentum, rows, width)


def near_groups(mesh):
    replicas, shards = mesh.shape["rep"], mesh.shape["fsdp"]

    def index(y, z, core, x):
        return ((y * 4 + z % 4) * 2 + core) * shards + x * 2 + z // 4

    partner = {0: 6, 1: 7, 2: 4, 3: 5}
    return [
        [index(y, z, core, x) for x in range(shards // 2) for z in (low, partner[low])]
        for y in range(replicas // 8)
        for low in range(4)
        for core in range(2)
    ]


def solution(mesh):
    groups = near_groups(mesh)
    return jax.shard_map(
        lambda *arrays: per_device(groups, *arrays),
        mesh=mesh,
        in_specs=(P("rep", "fsdp", None), P("fsdp", None), P("fsdp", None)),
        out_specs=(P("fsdp", None), P("fsdp", None)),
        check_vma=False,
    )
```

```python
import math

import jax
import jax.numpy as jnp
from jax import lax
from jax.experimental import pallas as pl
from jax.experimental.pallas import tpu as pltpu
from jax.sharding import PartitionSpec as P

QBLOCK = 32
LANES = 128
UNIT = 8
PARAMS = pltpu.CompilerParams(vmem_limit_bytes=4 << 20)

eps = 1e-06
clip_ratio = 0.2
outer_rate = 0.7
decay = 0.9

SUM_TYPE = jnp.float16
SUM_SCALE = 4.0

STAIR = (6.57973575592041, -12.987854957580566, 12.20757007598877, -6.687924861907959, 2.368926763534546, -0.5121700763702393)


def staircase(values):
    near = jnp.round(values)
    rest = values - near
    square = rest * rest
    poly = jnp.full_like(square, STAIR[-1])
    for coefficient in STAIR[-2::-1]:
        poly = poly * square + coefficient
    return near + rest * square * poly


def rounded(values):
    return values.astype(jnp.bfloat16).astype(jnp.float32)


def scale_of(top):
    return rounded((top + eps) * (1.0 / 7.0))


def code_of(values, scale):
    return rounded(staircase(values * pl.reciprocal(scale)))


def index_of(shape, axis):
    return lax.broadcasted_iota(jnp.int32, shape, axis)


def block_ones():
    shape = (LANES, LANES)
    return jnp.where(index_of(shape, 0) // QBLOCK == index_of(shape, 1) // QBLOCK, 1.0, 0.0).astype(jnp.bfloat16)


def spread(values, ones):
    return jnp.dot(values.astype(jnp.bfloat16), ones, preferred_element_type=jnp.float32)


def packed_top(arrays, lane):
    arrays = [jnp.abs(array) for array in arrays]
    shift = QBLOCK // 2
    while shift:
        if len(arrays) % 2:
            arrays.append(jnp.zeros_like(arrays[0]))
        halves = []
        for one, two in zip(arrays[::2], arrays[1::2]):
            one = jnp.maximum(one, pltpu.roll(one, shift, 1))
            two = jnp.maximum(two, pltpu.roll(two, LANES - shift, 1))
            halves.append(jnp.where(lane & shift != 0, one, two))
        arrays = halves
        shift //= 2
    return arrays[0]


def place_of(j):
    return sum((QBLOCK // 2) >> bit for bit in range(5) if not (j >> bit) & 1)


def full_top(values, lane):
    top = jnp.abs(values)
    for shift in (1, 4):
        down = [pltpu.roll(top, LANES - shift * k, 1) for k in (1, 2, 3)]
        up = [pltpu.roll(top, shift * k, 1) for k in (1, 2, 3)]
        place = (lane // shift) % 4
        first = jnp.where(place < 3, down[0], up[0])
        second = jnp.where(place < 2, down[1], up[1])
        third = jnp.where(place == 0, down[2], jnp.where(place == 3, up[2], up[0]))
        top = jnp.maximum(jnp.maximum(top, first), jnp.maximum(second, third))
    return jnp.maximum(top, jnp.where(lane < 16, pltpu.roll(top, LANES - 16, 1), pltpu.roll(top, 16, 1)))


def first_kernel(local_ref, base_ref, out_ref):
    rows = base_ref.shape[0] // UNIT
    ones = block_ones()
    lane = index_of((UNIT, LANES), 1) % QBLOCK
    mine = lax.rem(lax.axis_index("rep"), UNIT)
    base = base_ref[pl.ds(pl.multiple_of(mine * rows, UNIT), rows)]
    local = local_ref[...].astype(jnp.float32)
    starts = range(0, rows, UNIT)
    deltas = [base[i : i + UNIT] - local[j * rows + i : j * rows + i + UNIT] for j in range(UNIT) for i in starts]
    scales = []
    for first in range(0, len(deltas), QBLOCK):
        group = deltas[first : first + QBLOCK]
        scale = scale_of(packed_top(group, lane))
        scales += [jnp.where(lane == place_of(j), scale, 0.0) for j in range(len(group))]
    total = jnp.zeros((rows, LANES), jnp.float32)
    count = len(starts)
    for j in range(UNIT):
        here = slice(j * count, (j + 1) * count)
        scale = spread(jnp.concatenate(scales[here], axis=0), ones)
        total += code_of(jnp.concatenate(deltas[here], axis=0), scale) * scale
    total *= SUM_SCALE
    for j in range(UNIT):
        out_ref[j * rows : (j + 1) * rows] = total


def second_kernel(in_ref, out_ref, *, replicas):
    rows = in_ref.shape[0] // UNIT
    total = in_ref[:rows]
    for j in range(1, UNIT):
        total += in_ref[j * rows : (j + 1) * rows]
    average = total * (1.0 / (replicas * SUM_SCALE))
    lane = index_of(average.shape, 1) % QBLOCK
    row = index_of(average.shape, 0) % UNIT
    scale = scale_of(full_top(average, lane))
    code = code_of(average, scale)
    own = jnp.where(lane == row, scale, 0.0)
    place = index_of((UNIT, LANES), 0)
    lines = jnp.zeros((UNIT, LANES), jnp.float32)
    for i in range(rows // UNIT):
        line = jnp.sum(own[i * UNIT : (i + 1) * UNIT], axis=0, keepdims=True)
        lines = jnp.where(place == i, line, lines)
    message = jnp.concatenate([code, lines], axis=0).astype(jnp.bfloat16)
    size = rows + UNIT
    for j in range(UNIT):
        out_ref[j * size : (j + 1) * size] = message


def third_kernel(in_ref, grad_ref, squares_ref):
    ones = block_ones()
    size, rows = in_ref.shape[0] // UNIT, grad_ref.shape[0] // UNIT
    shape = (UNIT, LANES)
    own = index_of(shape, 0) == index_of(shape, 1) % QBLOCK
    total = jnp.zeros(shape, jnp.float32)
    for j in range(UNIT):
        message = in_ref[j * size : (j + 1) * size].astype(jnp.float32)
        scales = [
            jnp.where(own, jnp.broadcast_to(message[rows + i : rows + i + 1], shape), 0.0) for i in range(rows // UNIT)
        ]
        values = message[:rows] * spread(jnp.concatenate(scales, axis=0), ones)
        grad_ref[j * rows : (j + 1) * rows] = values
        total += jnp.sum((values * values).reshape(rows // UNIT, UNIT, LANES), axis=0)
    squares_ref[...] = jnp.full(shape, jnp.sum(total), jnp.float32)


def fourth_kernel(grad_ref, base_ref, momentum_ref, squares_ref, new_base_ref, new_momentum_ref, *, limit):
    squares = jnp.sum(squares_ref[...], axis=0, keepdims=True)
    factor = limit / jnp.maximum(jnp.sqrt(squares), limit)
    scaled = factor * grad_ref[...]
    momentum = decay * momentum_ref[...] + scaled
    new_momentum_ref[...] = momentum
    new_base_ref[...] = base_ref[...] - outer_rate * (scaled + decay * momentum)


def to_units(array):
    rows, width = array.shape
    return array.reshape(rows, width // LANES, LANES).transpose(1, 0, 2).reshape(rows * width // LANES, LANES)


def from_units(array, rows, width):
    return array.reshape(width // LANES, rows, LANES).transpose(1, 0, 2).reshape(rows, width)


def call(kernel, name, out_shape, *operands):
    return pl.pallas_call(kernel, name=name, compiler_params=PARAMS, out_shape=out_shape)(*operands)


def per_device(groups, local_params, base, momentum):
    replicas = lax.axis_size("rep")
    shards = lax.axis_size("fsdp")
    rows, width = base.shape
    units = rows * width // LANES
    planes = [[y * UNIT + q for q in range(UNIT)] for y in range(replicas // UNIT)]
    lines = [[y * UNIT + q for y in range(replicas // UNIT)] for q in range(UNIT)]

    def exchange(array, peers):
        return lax.all_to_all(array, "rep", split_axis=0, concat_axis=0, tiled=True, axis_index_groups=peers)

    def shape(count, dtype=jnp.float32):
        return jax.ShapeDtypeStruct((count, LANES), dtype)

    base_units = to_units(base)
    local = local_params[0].reshape(rows, width // LANES, LANES).transpose(1, 0, 2)
    local = exchange(local, planes).reshape(units, LANES)
    sums = call(first_kernel, "quantize_and_add", shape(units), local, base_units)
    sums = exchange(sums.astype(SUM_TYPE).reshape(UNIT, units // UNIT, LANES), lines)
    sums = sums.reshape(units, LANES).astype(jnp.float32)
    size = units // UNIT + UNIT
    message = call(lambda *refs: second_kernel(*refs, replicas=replicas), "average_and_encode", shape(UNIT * size, jnp.bfloat16), sums)
    message = exchange(message.reshape(UNIT, size, LANES), planes).reshape(UNIT * size, LANES)
    grad, squares = call(third_kernel, "decode_all", (shape(units), shape(shards)), message)
    squares = lax.all_to_all(
        squares.reshape(shards, 1, LANES), ("rep", "fsdp"), split_axis=0, concat_axis=0, tiled=True, axis_index_groups=groups
    ).reshape(shards, LANES)
    limit = clip_ratio * float(rows * width * shards) ** 0.5
    new_base, new_momentum = call(
        lambda *refs: fourth_kernel(*refs, limit=limit),
        "update",
        (shape(units), shape(units)),
        grad,
        base_units,
        to_units(momentum),
        squares,
    )
    return from_units(new_base, rows, width), from_units(new_momentum, rows, width)


def near_groups(mesh):
    replicas, shards = mesh.shape["rep"], mesh.shape["fsdp"]

    def index(y, z, core, x):
        return ((y * 4 + z % 4) * 2 + core) * shards + x * 2 + z // 4

    partner = {0: 6, 1: 7, 2: 4, 3: 5}
    return [
        [index(y, z, core, x) for x in range(shards // 2) for z in (low, partner[low])]
        for y in range(replicas // 8)
        for low in range(4)
        for core in range(2)
    ]


def solution(mesh):
    groups = near_groups(mesh)
    return jax.shard_map(
        lambda *arrays: per_device(groups, *arrays),
        mesh=mesh,
        in_specs=(P("rep", "fsdp", None), P("fsdp", None), P("fsdp", None)),
        out_specs=(P("fsdp", None), P("fsdp", None)),
        check_vma=False,
    )
```

```python
import math

import jax
import jax.numpy as jnp
from jax import lax
from jax.experimental import pallas as pl
from jax.experimental.pallas import tpu as pltpu
from jax.sharding import PartitionSpec as P

QBLOCK = 32
LANES = 128
UNIT = 8
PARAMS = pltpu.CompilerParams(vmem_limit_bytes=4 << 20)

eps = 1e-06
clip_ratio = 0.2
outer_rate = 0.7
decay = 0.9

SENT = jnp.float16
SUM_FACTOR = 512.0
GRAD_FACTOR = 1024.0

STAIR = (6.57973575592041, -12.987854957580566, 12.20757007598877, -6.687924861907959, 2.368926763534546, -0.5121700763702393)


def staircase(values):
    near = jnp.round(values)
    rest = values - near
    square = rest * rest
    poly = jnp.full_like(square, STAIR[-1])
    for coefficient in STAIR[-2::-1]:
        poly = poly * square + coefficient
    return near + rest * square * poly


def rounded(values):
    return values.astype(jnp.bfloat16).astype(jnp.float32)


def scale_of(top):
    return rounded((top + eps) * (1.0 / 7.0))


def code_of(values, scale):
    return rounded(staircase(values * pl.reciprocal(scale)))


def to_root(values, factor):
    root = jnp.sqrt(jnp.abs(values)) * factor
    return jnp.where(values < 0.0, -root, root)


def from_root(root, factor):
    root = root * (1.0 / factor)
    return root * jnp.abs(root)


def index_of(shape, axis):
    return lax.broadcasted_iota(jnp.int32, shape, axis)


def block_ones():
    shape = (LANES, LANES)
    return jnp.where(index_of(shape, 0) // QBLOCK == index_of(shape, 1) // QBLOCK, 1.0, 0.0).astype(jnp.bfloat16)


def spread(values, ones):
    return jnp.dot(values.astype(jnp.bfloat16), ones, preferred_element_type=jnp.float32)


def packed_top(arrays, lane):
    arrays = [jnp.abs(array) for array in arrays]
    shift = QBLOCK // 2
    while shift:
        if len(arrays) % 2:
            arrays.append(jnp.zeros_like(arrays[0]))
        halves = []
        for one, two in zip(arrays[::2], arrays[1::2]):
            one = jnp.maximum(one, pltpu.roll(one, shift, 1))
            two = jnp.maximum(two, pltpu.roll(two, LANES - shift, 1))
            halves.append(jnp.where(lane & shift != 0, one, two))
        arrays = halves
        shift //= 2
    return arrays[0]


def place_of(j):
    return sum((QBLOCK // 2) >> bit for bit in range(5) if not (j >> bit) & 1)


def full_top(values, lane):
    top = jnp.abs(values)
    for shift in (1, 4):
        down = [pltpu.roll(top, LANES - shift * k, 1) for k in (1, 2, 3)]
        up = [pltpu.roll(top, shift * k, 1) for k in (1, 2, 3)]
        place = (lane // shift) % 4
        first = jnp.where(place < 3, down[0], up[0])
        second = jnp.where(place < 2, down[1], up[1])
        third = jnp.where(place == 0, down[2], jnp.where(place == 3, up[2], up[0]))
        top = jnp.maximum(jnp.maximum(top, first), jnp.maximum(second, third))
    return jnp.maximum(top, jnp.where(lane < 16, pltpu.roll(top, LANES - 16, 1), pltpu.roll(top, 16, 1)))


def first_kernel(local_ref, base_ref, out_ref):
    rows = base_ref.shape[0] // UNIT
    ones = block_ones()
    lane = index_of((UNIT, LANES), 1) % QBLOCK
    mine = lax.rem(lax.axis_index("rep"), UNIT)
    base = base_ref[pl.ds(pl.multiple_of(mine * rows, UNIT), rows)]
    local = local_ref[...].astype(jnp.float32)
    starts = range(0, rows, UNIT)
    deltas = [base[i : i + UNIT] - local[j * rows + i : j * rows + i + UNIT] for j in range(UNIT) for i in starts]
    scales = []
    for first in range(0, len(deltas), QBLOCK):
        group = deltas[first : first + QBLOCK]
        scale = scale_of(packed_top(group, lane))
        scales += [jnp.where(lane == place_of(j), scale, 0.0) for j in range(len(group))]
    total = jnp.zeros((rows, LANES), jnp.float32)
    count = len(starts)
    for j in range(UNIT):
        here = slice(j * count, (j + 1) * count)
        scale = spread(jnp.concatenate(scales[here], axis=0), ones)
        total += code_of(jnp.concatenate(deltas[here], axis=0), scale) * scale
    total = to_root(total, SUM_FACTOR)
    for j in range(UNIT):
        out_ref[j * rows : (j + 1) * rows] = total


def second_kernel(in_ref, out_ref, *, replicas):
    rows = in_ref.shape[0] // UNIT
    total = from_root(in_ref[:rows], SUM_FACTOR)
    for j in range(1, UNIT):
        total += from_root(in_ref[j * rows : (j + 1) * rows], SUM_FACTOR)
    average = total * (1.0 / replicas)
    scale = scale_of(full_top(average, index_of(average.shape, 1) % QBLOCK))
    message = to_root(code_of(average, scale) * scale, GRAD_FACTOR)
    for j in range(UNIT):
        out_ref[j * rows : (j + 1) * rows] = message


def third_kernel(in_ref, grad_ref, squares_ref):
    grad = from_root(in_ref[...], GRAD_FACTOR)
    grad_ref[...] = grad
    total = jnp.sum((grad * grad).reshape(-1, UNIT, LANES), axis=0)
    squares_ref[...] = jnp.full((UNIT, LANES), jnp.sum(total), jnp.float32)


def fourth_kernel(grad_ref, base_ref, momentum_ref, squares_ref, new_base_ref, new_momentum_ref, *, limit):
    squares = jnp.sum(squares_ref[...], axis=0, keepdims=True)
    factor = limit / jnp.maximum(jnp.sqrt(squares), limit)
    scaled = factor * grad_ref[...]
    momentum = decay * momentum_ref[...] + scaled
    new_momentum_ref[...] = momentum
    new_base_ref[...] = base_ref[...] - outer_rate * (scaled + decay * momentum)


def to_units(array):
    rows, width = array.shape
    return array.reshape(rows, width // LANES, LANES).transpose(1, 0, 2).reshape(rows * width // LANES, LANES)


def from_units(array, rows, width):
    return array.reshape(width // LANES, rows, LANES).transpose(1, 0, 2).reshape(rows, width)


def call(kernel, name, out_shape, *operands):
    return pl.pallas_call(kernel, name=name, compiler_params=PARAMS, out_shape=out_shape)(*operands)


def per_device(groups, local_params, base, momentum):
    replicas = lax.axis_size("rep")
    shards = lax.axis_size("fsdp")
    rows, width = base.shape
    units = rows * width // LANES
    planes = [[y * UNIT + q for q in range(UNIT)] for y in range(replicas // UNIT)]
    lines = [[y * UNIT + q for y in range(replicas // UNIT)] for q in range(UNIT)]

    def exchange(array, peers):
        return lax.all_to_all(array, "rep", split_axis=0, concat_axis=0, tiled=True, axis_index_groups=peers)

    def exchange_roots(array, peers):
        array = exchange(array.astype(SENT).reshape(UNIT, units // UNIT, LANES), peers)
        return array.reshape(units, LANES).astype(jnp.float32)

    def shape(count):
        return jax.ShapeDtypeStruct((count, LANES), jnp.float32)

    base_units = to_units(base)
    local = local_params[0].reshape(rows, width // LANES, LANES).transpose(1, 0, 2)
    local = exchange(local, planes).reshape(units, LANES)
    sums = call(first_kernel, "quantize_and_add", shape(units), local, base_units)
    sums = exchange_roots(sums, lines)
    parts = call(lambda *refs: second_kernel(*refs, replicas=replicas), "average_and_quantize", shape(units), sums)
    parts = exchange_roots(parts, planes)
    grad, squares = call(third_kernel, "grad_and_squares", (shape(units), shape(shards)), parts)
    squares = lax.all_to_all(
        squares.reshape(shards, 1, LANES), ("rep", "fsdp"), split_axis=0, concat_axis=0, tiled=True, axis_index_groups=groups
    ).reshape(shards, LANES)
    limit = clip_ratio * float(rows * width * shards) ** 0.5
    new_base, new_momentum = call(
        lambda *refs: fourth_kernel(*refs, limit=limit),
        "update",
        (shape(units), shape(units)),
        grad,
        base_units,
        to_units(momentum),
        squares,
    )
    return from_units(new_base, rows, width), from_units(new_momentum, rows, width)


def near_groups(mesh):
    replicas, shards = mesh.shape["rep"], mesh.shape["fsdp"]

    def index(y, z, core, x):
        return ((y * 4 + z % 4) * 2 + core) * shards + x * 2 + z // 4

    partner = {0: 6, 1: 7, 2: 4, 3: 5}
    return [
        [index(y, z, core, x) for x in range(shards // 2) for z in (low, partner[low])]
        for y in range(replicas // 8)
        for low in range(4)
        for core in range(2)
    ]


def solution(mesh):
    groups = near_groups(mesh)
    return jax.shard_map(
        lambda *arrays: per_device(groups, *arrays),
        mesh=mesh,
        in_specs=(P("rep", "fsdp", None), P("fsdp", None), P("fsdp", None)),
        out_specs=(P("fsdp", None), P("fsdp", None)),
        check_vma=False,
    )
```

```python
import math

import jax
import jax.numpy as jnp
from jax import lax
from jax.experimental import pallas as pl
from jax.experimental.pallas import tpu as pltpu
from jax.sharding import PartitionSpec as P

QBLOCK = 32
LANES = 128
UNIT = 8
PARAMS = pltpu.CompilerParams(vmem_limit_bytes=4 << 20)

eps = 1e-06
clip_ratio = 0.2
outer_rate = 0.7
decay = 0.9

SENT = jnp.float16
SUM_FACTOR = 512.0
GRAD_FACTOR = 1024.0

STAIR = (6.57973575592041, -12.987854957580566, 12.20757007598877, -6.687924861907959, 2.368926763534546, -0.5121700763702393)


def staircase(values):
    near = jnp.round(values)
    rest = values - near
    square = rest * rest
    poly = jnp.full_like(square, STAIR[-1])
    for coefficient in STAIR[-2::-1]:
        poly = poly * square + coefficient
    return near + rest * square * poly


def rounded(values):
    return values.astype(jnp.bfloat16).astype(jnp.float32)


def scale_of(top):
    return rounded((top + eps) * (1.0 / 7.0))


def code_of(values, scale):
    return rounded(staircase(values * pl.reciprocal(scale)))


def to_root(values, factor):
    root = jnp.sqrt(jnp.abs(values)) * factor
    return jnp.where(values < 0.0, -root, root)


def from_root(root, factor):
    root = root * (1.0 / factor)
    return root * jnp.abs(root)


def index_of(shape, axis):
    return lax.broadcasted_iota(jnp.int32, shape, axis)


def block_ones():
    shape = (LANES, LANES)
    return jnp.where(index_of(shape, 0) // QBLOCK == index_of(shape, 1) // QBLOCK, 1.0, 0.0).astype(jnp.bfloat16)


def spread(values, ones):
    return jnp.dot(values.astype(jnp.bfloat16), ones, preferred_element_type=jnp.float32)


def packed_top(arrays, lane):
    arrays = [jnp.abs(array) for array in arrays]
    shift = QBLOCK // 2
    while shift:
        if len(arrays) % 2:
            arrays.append(jnp.zeros_like(arrays[0]))
        halves = []
        for one, two in zip(arrays[::2], arrays[1::2]):
            one = jnp.maximum(one, pltpu.roll(one, shift, 1))
            two = jnp.maximum(two, pltpu.roll(two, LANES - shift, 1))
            halves.append(jnp.where(lane & shift != 0, one, two))
        arrays = halves
        shift //= 2
    return arrays[0]


def place_of(j):
    return sum((QBLOCK // 2) >> bit for bit in range(5) if not (j >> bit) & 1)


def full_top(values, lane):
    top = jnp.abs(values)
    for shift in (1, 4):
        down = [pltpu.roll(top, LANES - shift * k, 1) for k in (1, 2, 3)]
        up = [pltpu.roll(top, shift * k, 1) for k in (1, 2, 3)]
        place = (lane // shift) % 4
        first = jnp.where(place < 3, down[0], up[0])
        second = jnp.where(place < 2, down[1], up[1])
        third = jnp.where(place == 0, down[2], jnp.where(place == 3, up[2], up[0]))
        top = jnp.maximum(jnp.maximum(top, first), jnp.maximum(second, third))
    return jnp.maximum(top, jnp.where(lane < 16, pltpu.roll(top, LANES - 16, 1), pltpu.roll(top, 16, 1)))


def place_in_cell(rep):
    return lax.rem(rep // 8, 2) * 4 + lax.rem(rep // 2, 2) * 2 + lax.rem(rep, 2)


def first_kernel(local_ref, base_ref, out_ref):
    rows = base_ref.shape[0] // UNIT
    ones = block_ones()
    lane = index_of((UNIT, LANES), 1) % QBLOCK
    mine = place_in_cell(lax.axis_index("rep"))
    base = base_ref[pl.ds(pl.multiple_of(mine * rows, UNIT), rows)]
    local = local_ref[...].astype(jnp.float32)
    starts = range(0, rows, UNIT)
    deltas = [base[i : i + UNIT] - local[j * rows + i : j * rows + i + UNIT] for j in range(UNIT) for i in starts]
    scales = []
    for first in range(0, len(deltas), QBLOCK):
        group = deltas[first : first + QBLOCK]
        scale = scale_of(packed_top(group, lane))
        scales += [jnp.where(lane == place_of(j), scale, 0.0) for j in range(len(group))]
    total = jnp.zeros((rows, LANES), jnp.float32)
    count = len(starts)
    for j in range(UNIT):
        here = slice(j * count, (j + 1) * count)
        scale = spread(jnp.concatenate(scales[here], axis=0), ones)
        total += code_of(jnp.concatenate(deltas[here], axis=0), scale) * scale
    total = to_root(total, SUM_FACTOR)
    for j in range(UNIT):
        out_ref[j * rows : (j + 1) * rows] = total


def second_kernel(in_ref, out_ref, *, replicas):
    rows = in_ref.shape[0] // UNIT
    total = from_root(in_ref[:rows], SUM_FACTOR)
    for j in range(1, UNIT):
        total += from_root(in_ref[j * rows : (j + 1) * rows], SUM_FACTOR)
    average = total * (1.0 / replicas)
    scale = scale_of(full_top(average, index_of(average.shape, 1) % QBLOCK))
    message = to_root(code_of(average, scale) * scale, GRAD_FACTOR)
    for j in range(UNIT):
        out_ref[j * rows : (j + 1) * rows] = message


def third_kernel(in_ref, grad_ref, squares_ref):
    grad = from_root(in_ref[...], GRAD_FACTOR)
    grad_ref[...] = grad
    total = jnp.sum((grad * grad).reshape(-1, UNIT, LANES), axis=0)
    squares_ref[...] = jnp.full((UNIT, LANES), jnp.sum(total), jnp.float32)


def fourth_kernel(grad_ref, base_ref, momentum_ref, squares_ref, new_base_ref, new_momentum_ref, *, limit):
    squares = jnp.sum(squares_ref[...], axis=0, keepdims=True)
    factor = limit / jnp.maximum(jnp.sqrt(squares), limit)
    scaled = factor * grad_ref[...]
    momentum = decay * momentum_ref[...] + scaled
    new_momentum_ref[...] = momentum
    new_base_ref[...] = base_ref[...] - outer_rate * (scaled + decay * momentum)


def to_units(array):
    rows, width = array.shape
    return array.reshape(rows, width // LANES, LANES).transpose(1, 0, 2).reshape(rows * width // LANES, LANES)


def from_units(array, rows, width):
    return array.reshape(width // LANES, rows, LANES).transpose(1, 0, 2).reshape(rows, width)


def call(kernel, name, out_shape, *operands):
    return pl.pallas_call(kernel, name=name, compiler_params=PARAMS, out_shape=out_shape)(*operands)


def per_device(groups, local_params, base, momentum):
    replicas = lax.axis_size("rep")
    shards = lax.axis_size("fsdp")
    rows, width = base.shape
    units = rows * width // LANES
    cells, across = cell_groups()

    def exchange(array, peers):
        return lax.all_to_all(array, "rep", split_axis=0, concat_axis=0, tiled=True, axis_index_groups=peers)

    def exchange_roots(array, peers):
        array = exchange(array.astype(SENT).reshape(UNIT, units // UNIT, LANES), peers)
        return array.reshape(units, LANES).astype(jnp.float32)

    def shape(count):
        return jax.ShapeDtypeStruct((count, LANES), jnp.float32)

    base_units = to_units(base)
    local = local_params[0].reshape(rows, width // LANES, LANES).transpose(1, 0, 2)
    local = exchange(local, cells).reshape(units, LANES)
    sums = call(first_kernel, "quantize_and_add", shape(units), local, base_units)
    sums = exchange_roots(sums, across)
    parts = call(lambda *refs: second_kernel(*refs, replicas=replicas), "average_and_quantize", shape(units), sums)
    parts = exchange_roots(parts, cells)
    grad, squares = call(third_kernel, "grad_and_squares", (shape(units), shape(shards)), parts)
    squares = lax.all_to_all(
        squares.reshape(shards, 1, LANES), ("rep", "fsdp"), split_axis=0, concat_axis=0, tiled=True, axis_index_groups=groups
    ).reshape(shards, LANES)
    limit = clip_ratio * float(rows * width * shards) ** 0.5
    new_base, new_momentum = call(
        lambda *refs: fourth_kernel(*refs, limit=limit),
        "update",
        (shape(units), shape(units)),
        grad,
        base_units,
        to_units(momentum),
        squares,
    )
    return from_units(new_base, rows, width), from_units(new_momentum, rows, width)


def cell_groups():
    cells = [
        [((2 * y + a) * 4 + 2 * z + b) * 2 + core for a in range(2) for b in range(2) for core in range(2)]
        for y in range(4)
        for z in range(2)
    ]
    return cells, [list(group) for group in zip(*cells)]


def near_groups(mesh):
    replicas, shards = mesh.shape["rep"], mesh.shape["fsdp"]

    def index(y, z, core, x):
        return ((y * 4 + z % 4) * 2 + core) * shards + x * 2 + z // 4

    partner = {0: 6, 1: 7, 2: 4, 3: 5}
    return [
        [index(y, z, core, x) for x in range(shards // 2) for z in (low, partner[low])]
        for y in range(replicas // 8)
        for low in range(4)
        for core in range(2)
    ]


def solution(mesh):
    groups = near_groups(mesh)
    return jax.shard_map(
        lambda *arrays: per_device(groups, *arrays),
        mesh=mesh,
        in_specs=(P("rep", "fsdp", None), P("fsdp", None), P("fsdp", None)),
        out_specs=(P("fsdp", None), P("fsdp", None)),
        check_vma=False,
    )
```

```python
import math

import jax
import jax.numpy as jnp
from jax import lax
from jax.experimental import pallas as pl
from jax.experimental.pallas import tpu as pltpu
from jax.sharding import PartitionSpec as P

QBLOCK = 32
LANES = 128
UNIT = 8
PARAMS = pltpu.CompilerParams(vmem_limit_bytes=4 << 20)

eps = 1e-06
clip_ratio = 0.2
outer_rate = 0.7
decay = 0.9

SENT = jnp.float16
SUM_FACTOR = 512.0
GRAD_FACTOR = 1024.0

STAIR = (6.57973575592041, -12.987854957580566, 12.20757007598877, -6.687924861907959, 2.368926763534546, -0.5121700763702393)


def staircase(values):
    near = jnp.round(values)
    rest = values - near
    square = rest * rest
    poly = jnp.full_like(square, STAIR[-1])
    for coefficient in STAIR[-2::-1]:
        poly = poly * square + coefficient
    return near + rest * square * poly


def rounded(values):
    return values.astype(jnp.bfloat16).astype(jnp.float32)


def scale_of(top):
    return rounded((top + eps) * (1.0 / 7.0))


def code_of(values, scale):
    return rounded(staircase(values * pl.reciprocal(scale)))


def to_root(values, factor):
    root = jnp.sqrt(jnp.abs(values)) * factor
    return jnp.where(values < 0.0, -root, root)


def from_root(root, factor):
    root = root * (1.0 / factor)
    return root * jnp.abs(root)


def index_of(shape, axis):
    return lax.broadcasted_iota(jnp.int32, shape, axis)


def block_ones():
    shape = (LANES, LANES)
    return jnp.where(index_of(shape, 0) // QBLOCK == index_of(shape, 1) // QBLOCK, 1.0, 0.0).astype(jnp.bfloat16)


def spread(values, ones):
    return jnp.dot(values.astype(jnp.bfloat16), ones, preferred_element_type=jnp.float32)


def packed_top(arrays, lane):
    arrays = [jnp.abs(array) for array in arrays]
    shift = QBLOCK // 2
    while shift:
        if len(arrays) % 2:
            arrays.append(jnp.zeros_like(arrays[0]))
        halves = []
        for one, two in zip(arrays[::2], arrays[1::2]):
            one = jnp.maximum(one, pltpu.roll(one, shift, 1))
            two = jnp.maximum(two, pltpu.roll(two, LANES - shift, 1))
            halves.append(jnp.where(lane & shift != 0, one, two))
        arrays = halves
        shift //= 2
    return arrays[0]


def place_of(j):
    return sum((QBLOCK // 2) >> bit for bit in range(5) if not (j >> bit) & 1)


def full_top(values, lane):
    top = jnp.abs(values)
    for shift in (1, 4):
        down = [pltpu.roll(top, LANES - shift * k, 1) for k in (1, 2, 3)]
        up = [pltpu.roll(top, shift * k, 1) for k in (1, 2, 3)]
        place = (lane // shift) % 4
        first = jnp.where(place < 3, down[0], up[0])
        second = jnp.where(place < 2, down[1], up[1])
        third = jnp.where(place == 0, down[2], jnp.where(place == 3, up[2], up[0]))
        top = jnp.maximum(jnp.maximum(top, first), jnp.maximum(second, third))
    return jnp.maximum(top, jnp.where(lane < 16, pltpu.roll(top, LANES - 16, 1), pltpu.roll(top, 16, 1)))


def place_in_cell(rep):
    return lax.rem(rep // 8 + rep // 32, 2) * 4 + lax.rem(rep // 2, 2) * 2 + lax.rem(rep, 2)


def first_kernel(local_ref, base_ref, out_ref):
    rows = base_ref.shape[0] // UNIT
    ones = block_ones()
    lane = index_of((UNIT, LANES), 1) % QBLOCK
    mine = place_in_cell(lax.axis_index("rep"))
    base = base_ref[pl.ds(pl.multiple_of(mine * rows, UNIT), rows)]
    local = local_ref[...].astype(jnp.float32)
    starts = range(0, rows, UNIT)
    deltas = [base[i : i + UNIT] - local[j * rows + i : j * rows + i + UNIT] for j in range(UNIT) for i in starts]
    scales = []
    for first in range(0, len(deltas), QBLOCK):
        group = deltas[first : first + QBLOCK]
        scale = scale_of(packed_top(group, lane))
        scales += [jnp.where(lane == place_of(j), scale, 0.0) for j in range(len(group))]
    total = jnp.zeros((rows, LANES), jnp.float32)
    count = len(starts)
    for j in range(UNIT):
        here = slice(j * count, (j + 1) * count)
        scale = spread(jnp.concatenate(scales[here], axis=0), ones)
        total += code_of(jnp.concatenate(deltas[here], axis=0), scale) * scale
    total = to_root(total, SUM_FACTOR)
    for j in range(UNIT):
        out_ref[j * rows : (j + 1) * rows] = total


def second_kernel(in_ref, out_ref, *, replicas):
    rows = in_ref.shape[0] // UNIT
    total = from_root(in_ref[:rows], SUM_FACTOR)
    for j in range(1, UNIT):
        total += from_root(in_ref[j * rows : (j + 1) * rows], SUM_FACTOR)
    average = total * (1.0 / replicas)
    scale = scale_of(full_top(average, index_of(average.shape, 1) % QBLOCK))
    message = to_root(code_of(average, scale) * scale, GRAD_FACTOR)
    for j in range(UNIT):
        out_ref[j * rows : (j + 1) * rows] = message


def third_kernel(in_ref, grad_ref, squares_ref):
    grad = from_root(in_ref[...], GRAD_FACTOR)
    grad_ref[...] = grad
    total = jnp.sum((grad * grad).reshape(-1, UNIT, LANES), axis=0)
    squares_ref[...] = jnp.full((UNIT, LANES), jnp.sum(total), jnp.float32)


def fourth_kernel(grad_ref, base_ref, momentum_ref, squares_ref, new_base_ref, new_momentum_ref, *, limit):
    squares = jnp.sum(squares_ref[...], axis=0, keepdims=True)
    factor = limit / jnp.maximum(jnp.sqrt(squares), limit)
    scaled = factor * grad_ref[...]
    momentum = decay * momentum_ref[...] + scaled
    new_momentum_ref[...] = momentum
    new_base_ref[...] = base_ref[...] - outer_rate * (scaled + decay * momentum)


def to_units(array):
    rows, width = array.shape
    return array.reshape(rows, width // LANES, LANES).transpose(1, 0, 2).reshape(rows * width // LANES, LANES)


def from_units(array, rows, width):
    return array.reshape(width // LANES, rows, LANES).transpose(1, 0, 2).reshape(rows, width)


def call(kernel, name, out_shape, *operands):
    return pl.pallas_call(kernel, name=name, compiler_params=PARAMS, out_shape=out_shape)(*operands)


def per_device(groups, local_params, base, momentum):
    replicas = lax.axis_size("rep")
    shards = lax.axis_size("fsdp")
    rows, width = base.shape
    units = rows * width // LANES
    cells, across = cell_groups()

    def exchange(array, peers):
        return lax.all_to_all(array, "rep", split_axis=0, concat_axis=0, tiled=True, axis_index_groups=peers)

    def exchange_roots(array, peers):
        array = exchange(array.astype(SENT).reshape(UNIT, units // UNIT, LANES), peers)
        return array.reshape(units, LANES).astype(jnp.float32)

    def shape(count):
        return jax.ShapeDtypeStruct((count, LANES), jnp.float32)

    base_units = to_units(base)
    local = local_params[0].reshape(rows, width // LANES, LANES).transpose(1, 0, 2)
    local = exchange(local, cells).reshape(units, LANES)
    sums = call(first_kernel, "quantize_and_add", shape(units), local, base_units)
    sums = exchange_roots(sums, across)
    parts = call(lambda *refs: second_kernel(*refs, replicas=replicas), "average_and_quantize", shape(units), sums)
    parts = exchange_roots(parts, cells)
    grad, squares = call(third_kernel, "grad_and_squares", (shape(units), shape(shards)), parts)
    squares = lax.all_to_all(
        squares.reshape(shards, 1, LANES), ("rep", "fsdp"), split_axis=0, concat_axis=0, tiled=True, axis_index_groups=groups
    ).reshape(shards, LANES)
    limit = clip_ratio * float(rows * width * shards) ** 0.5
    new_base, new_momentum = call(
        lambda *refs: fourth_kernel(*refs, limit=limit),
        "update",
        (shape(units), shape(units)),
        grad,
        base_units,
        to_units(momentum),
        squares,
    )
    return from_units(new_base, rows, width), from_units(new_momentum, rows, width)


def cell_groups():
    cells = [
        [((2 * y + (a + y // 2) % 2) * 4 + 2 * z + b) * 2 + core for a in range(2) for b in range(2) for core in range(2)]
        for y in range(4)
        for z in range(2)
    ]
    return cells, [list(group) for group in zip(*cells)]


def near_groups(mesh):
    replicas, shards = mesh.shape["rep"], mesh.shape["fsdp"]

    def index(y, z, core, x):
        return ((y * 4 + z % 4) * 2 + core) * shards + x * 2 + z // 4

    partner = {0: 6, 1: 7, 2: 4, 3: 5}
    return [
        [index(y, z, core, x) for x in range(shards // 2) for z in (low, partner[low])]
        for y in range(replicas // 8)
        for low in range(4)
        for core in range(2)
    ]


def solution(mesh):
    groups = near_groups(mesh)
    return jax.shard_map(
        lambda *arrays: per_device(groups, *arrays),
        mesh=mesh,
        in_specs=(P("rep", "fsdp", None), P("fsdp", None), P("fsdp", None)),
        out_specs=(P("fsdp", None), P("fsdp", None)),
        check_vma=False,
    )
```

```python
import math

import jax
import jax.numpy as jnp
from jax import lax
from jax.experimental import pallas as pl
from jax.experimental.pallas import tpu as pltpu
from jax.sharding import PartitionSpec as P

QBLOCK = 32
LANES = 128
UNIT = 8
PARAMS = pltpu.CompilerParams(vmem_limit_bytes=4 << 20)

eps = 1e-06
clip_ratio = 0.2
outer_rate = 0.7
decay = 0.9

SENT = jnp.float16
SUM_FACTOR = 512.0
GRAD_FACTOR = 1024.0

STAIR = (6.57973575592041, -12.987854957580566, 12.20757007598877, -6.687924861907959, 2.368926763534546, -0.5121700763702393)


def staircase(values):
    near = jnp.round(values)
    rest = values - near
    square = rest * rest
    poly = jnp.full_like(square, STAIR[-1])
    for coefficient in STAIR[-2::-1]:
        poly = poly * square + coefficient
    return near + rest * square * poly


def rounded(values):
    return values.astype(jnp.bfloat16).astype(jnp.float32)


def scale_of(top):
    return rounded((top + eps) * (1.0 / 7.0))


def code_of(values, scale):
    return rounded(staircase(values * pl.reciprocal(scale)))


def to_root(values, factor):
    root = jnp.sqrt(jnp.abs(values)) * factor
    return jnp.where(values < 0.0, -root, root)


def from_root(root, factor):
    root = root * (1.0 / factor)
    return root * jnp.abs(root)


def index_of(shape, axis):
    return lax.broadcasted_iota(jnp.int32, shape, axis)


def block_ones():
    shape = (LANES, LANES)
    return jnp.where(index_of(shape, 0) // QBLOCK == index_of(shape, 1) // QBLOCK, 1.0, 0.0).astype(jnp.bfloat16)


def spread(values, ones):
    return jnp.dot(values.astype(jnp.bfloat16), ones, preferred_element_type=jnp.float32)


def merged_four(arrays, lane, unit):
    merged = None
    for k, array in enumerate(arrays):
        place = 3 - (k % 2 * 2 + k // 2)
        top = array
        for other in range(4):
            if other != place:
                top = jnp.maximum(top, pltpu.roll(array, (place - other) * unit % LANES, 1))
        merged = top if merged is None else jnp.where(lane // unit % 4 == place, top, merged)
    return merged


def packed_top(arrays, lane):
    arrays = [jnp.abs(array) for array in arrays]
    arrays += [jnp.zeros_like(arrays[0])] * (-len(arrays) % 8)
    half = QBLOCK // 2
    halves = []
    for one, two in zip(arrays[::2], arrays[1::2]):
        one = jnp.maximum(one, pltpu.roll(one, half, 1))
        two = jnp.maximum(two, pltpu.roll(two, LANES - half, 1))
        halves.append(jnp.where(lane >= half, one, two))
    arrays = [merged_four(halves[k : k + 4], lane, 4) for k in range(0, len(halves), 4)]
    arrays += [jnp.zeros_like(arrays[0])] * (4 - len(arrays))
    return merged_four(arrays, lane, 1)


def place_of(j):
    return sum((QBLOCK // 2) >> bit for bit in range(5) if not (j >> bit) & 1)


def full_top(values, lane):
    top = jnp.abs(values)
    for shift in (1, 4):
        down = [pltpu.roll(top, LANES - shift * k, 1) for k in (1, 2, 3)]
        up = [pltpu.roll(top, shift * k, 1) for k in (1, 2, 3)]
        place = (lane // shift) % 4
        first = jnp.where(place < 3, down[0], up[0])
        second = jnp.where(place < 2, down[1], up[1])
        third = jnp.where(place == 0, down[2], jnp.where(place == 3, up[2], up[0]))
        top = jnp.maximum(jnp.maximum(top, first), jnp.maximum(second, third))
    return jnp.maximum(top, jnp.where(lane < 16, pltpu.roll(top, LANES - 16, 1), pltpu.roll(top, 16, 1)))


def place_in_cell(rep):
    return lax.rem(rep // 8 + rep // 32, 2) * 4 + lax.rem(rep // 2, 2) * 2 + lax.rem(rep + rep // 4, 2)


def first_kernel(local_ref, base_ref, out_ref):
    rows = base_ref.shape[0] // UNIT
    ones = block_ones()
    lane = index_of((UNIT, LANES), 1) % QBLOCK
    mine = place_in_cell(lax.axis_index("rep"))
    base = base_ref[pl.ds(pl.multiple_of(mine * rows, UNIT), rows)]
    local = local_ref[...].astype(jnp.float32)
    starts = range(0, rows, UNIT)
    deltas = [base[i : i + UNIT] - local[j * rows + i : j * rows + i + UNIT] for j in range(UNIT) for i in starts]
    scales = []
    for first in range(0, len(deltas), QBLOCK):
        group = deltas[first : first + QBLOCK]
        scale = scale_of(packed_top(group, lane))
        scales += [jnp.where(lane == place_of(j), scale, 0.0) for j in range(len(group))]
    total = jnp.zeros((rows, LANES), jnp.float32)
    count = len(starts)
    scale = spread(jnp.concatenate(scales, axis=0), ones)
    value = code_of(jnp.concatenate(deltas, axis=0), scale) * scale
    total = value[:rows]
    for j in range(1, UNIT):
        total += value[j * rows : (j + 1) * rows]
    total = to_root(total, SUM_FACTOR)
    for j in range(UNIT):
        out_ref[j * rows : (j + 1) * rows] = total


def second_kernel(in_ref, out_ref, *, replicas):
    rows = in_ref.shape[0] // UNIT
    total = from_root(in_ref[:rows], SUM_FACTOR)
    for j in range(1, UNIT):
        total += from_root(in_ref[j * rows : (j + 1) * rows], SUM_FACTOR)
    average = total * (1.0 / replicas)
    scale = scale_of(full_top(average, index_of(average.shape, 1) % QBLOCK))
    message = to_root(code_of(average, scale) * scale, GRAD_FACTOR)
    for j in range(UNIT):
        out_ref[j * rows : (j + 1) * rows] = message


def third_kernel(in_ref, squares_ref):
    grad = from_root(in_ref[...], GRAD_FACTOR)
    total = jnp.sum((grad * grad).reshape(-1, UNIT, LANES), axis=0)
    squares_ref[...] = jnp.broadcast_to(jnp.sum(total, axis=0, keepdims=True), (UNIT, LANES))


def fourth_kernel(parts_ref, base_ref, momentum_ref, squares_ref, new_base_ref, new_momentum_ref, *, limit):
    squares = jnp.sum(jnp.sum(squares_ref[...], axis=0, keepdims=True), axis=1, keepdims=True)
    factor = limit / jnp.maximum(jnp.sqrt(squares), limit)
    scaled = factor * from_root(parts_ref[...], GRAD_FACTOR)
    momentum = decay * momentum_ref[...] + scaled
    new_momentum_ref[...] = momentum
    new_base_ref[...] = base_ref[...] - outer_rate * (scaled + decay * momentum)


def to_units(array):
    rows, width = array.shape
    return array.reshape(rows, width // LANES, LANES).transpose(1, 0, 2).reshape(rows * width // LANES, LANES)


def from_units(array, rows, width):
    return array.reshape(width // LANES, rows, LANES).transpose(1, 0, 2).reshape(rows, width)


def call(kernel, name, out_shape, *operands):
    return pl.pallas_call(kernel, name=name, compiler_params=PARAMS, out_shape=out_shape)(*operands)


def per_device(groups, local_params, base, momentum):
    replicas = lax.axis_size("rep")
    shards = lax.axis_size("fsdp")
    rows, width = base.shape
    units = rows * width // LANES
    cells, across = cell_groups()

    def exchange(array, peers):
        return lax.all_to_all(array, "rep", split_axis=0, concat_axis=0, tiled=True, axis_index_groups=peers)

    def exchange_roots(array, peers):
        array = exchange(array.astype(SENT).reshape(UNIT, units // UNIT, LANES), peers)
        return array.reshape(units, LANES).astype(jnp.float32)

    def shape(count):
        return jax.ShapeDtypeStruct((count, LANES), jnp.float32)

    base_units = to_units(base)
    local = local_params[0].reshape(rows, width // LANES, LANES).transpose(1, 0, 2)
    local = exchange(local, cells).reshape(units, LANES)
    sums = call(first_kernel, "quantize_and_add", shape(units), local, base_units)
    sums = exchange_roots(sums, across)
    parts = call(lambda *refs: second_kernel(*refs, replicas=replicas), "average_and_quantize", shape(units), sums)
    parts = exchange_roots(parts, cells)
    squares = call(third_kernel, "add_squares", shape(shards), parts)
    squares = lax.all_to_all(
        squares.reshape(shards, 1, LANES), ("rep", "fsdp"), split_axis=0, concat_axis=0, tiled=True, axis_index_groups=groups
    ).reshape(shards, LANES)
    limit = clip_ratio * float(rows * width * shards) ** 0.5
    new_base, new_momentum = call(
        lambda *refs: fourth_kernel(*refs, limit=limit),
        "update",
        (shape(units), shape(units)),
        parts,
        base_units,
        to_units(momentum),
        squares,
    )
    return from_units(new_base, rows, width), from_units(new_momentum, rows, width)


def cell_groups():
    cells = [
        [((2 * y + (a + y // 2) % 2) * 4 + 2 * z + b) * 2 + (core + z) % 2 for a in range(2) for b in range(2) for core in range(2)]
        for y in range(4)
        for z in range(2)
    ]
    return cells, [list(group) for group in zip(*cells)]


def near_groups(mesh):
    replicas, shards = mesh.shape["rep"], mesh.shape["fsdp"]

    def index(y, z, core, x):
        return ((y * 4 + z % 4) * 2 + core) * shards + x * 2 + z // 4

    partner = {0: 6, 1: 7, 2: 4, 3: 5}
    return [
        [index(y, z, core, x) for x in range(shards // 2) for z in (low, partner[low])]
        for y in range(replicas // 8)
        for low in range(4)
        for core in range(2)
    ]


def solution(mesh):
    groups = near_groups(mesh)
    return jax.shard_map(
        lambda *arrays: per_device(groups, *arrays),
        mesh=mesh,
        in_specs=(P("rep", "fsdp", None), P("fsdp", None), P("fsdp", None)),
        out_specs=(P("fsdp", None), P("fsdp", None)),
        check_vma=False,
    )
```

```python
import math

import jax
import jax.numpy as jnp
from jax import lax
from jax.experimental import pallas as pl
from jax.experimental.pallas import tpu as pltpu
from jax.sharding import PartitionSpec as P

QBLOCK = 32
LANES = 128
UNIT = 8
PARAMS = pltpu.CompilerParams(vmem_limit_bytes=4 << 20)

eps = 1e-06
clip_ratio = 0.2
outer_rate = 0.7
decay = 0.9

SENT = jnp.float16
SUM_FACTOR = 512.0
GRAD_FACTOR = 1024.0

STAIR = (6.57973575592041, -12.987854957580566, 12.20757007598877, -6.687924861907959, 2.368926763534546, -0.5121700763702393)


def staircase(values):
    near = jnp.round(values)
    rest = values - near
    square = rest * rest
    poly = jnp.full_like(square, STAIR[-1])
    for coefficient in STAIR[-2::-1]:
        poly = poly * square + coefficient
    return near + rest * square * poly


def rounded(values):
    return values.astype(jnp.bfloat16).astype(jnp.float32)


def scale_of(top):
    return rounded((top + eps) * (1.0 / 7.0))


def code_of(values, scale):
    return rounded(staircase(values * pl.reciprocal(scale)))


def to_root(values, factor):
    root = jnp.sqrt(jnp.abs(values)) * factor
    return jnp.where(values < 0.0, -root, root)


def from_root(root, factor):
    root = root * (1.0 / factor)
    return root * jnp.abs(root)


def index_of(shape, axis):
    return lax.broadcasted_iota(jnp.int32, shape, axis)


def block_ones():
    shape = (LANES, LANES)
    return jnp.where(index_of(shape, 0) // QBLOCK == index_of(shape, 1) // QBLOCK, 1.0, 0.0).astype(jnp.bfloat16)


def spread(values, ones):
    return jnp.dot(values.astype(jnp.bfloat16), ones, preferred_element_type=jnp.float32)


def merged_four(arrays, lane, unit):
    merged = None
    for k, array in enumerate(arrays):
        place = 3 - (k % 2 * 2 + k // 2)
        top = array
        for other in range(4):
            if other != place:
                top = jnp.maximum(top, pltpu.roll(array, (place - other) * unit % LANES, 1))
        merged = top if merged is None else jnp.where(lane // unit % 4 == place, top, merged)
    return merged


def packed_top(arrays, lane):
    arrays = [jnp.abs(array) for array in arrays]
    arrays += [jnp.zeros_like(arrays[0])] * (-len(arrays) % 8)
    half = QBLOCK // 2
    halves = []
    for one, two in zip(arrays[::2], arrays[1::2]):
        one = jnp.maximum(one, pltpu.roll(one, half, 1))
        two = jnp.maximum(two, pltpu.roll(two, LANES - half, 1))
        halves.append(jnp.where(lane >= half, one, two))
    arrays = [merged_four(halves[k : k + 4], lane, 4) for k in range(0, len(halves), 4)]
    arrays += [jnp.zeros_like(arrays[0])] * (4 - len(arrays))
    return merged_four(arrays, lane, 1)


def place_of(j):
    return sum((QBLOCK // 2) >> bit for bit in range(5) if not (j >> bit) & 1)


def full_top(values, lane):
    top = jnp.abs(values)
    for shift in (1, 4):
        down = [pltpu.roll(top, LANES - shift * k, 1) for k in (1, 2, 3)]
        up = [pltpu.roll(top, shift * k, 1) for k in (1, 2, 3)]
        place = (lane // shift) % 4
        first = jnp.where(place < 3, down[0], up[0])
        second = jnp.where(place < 2, down[1], up[1])
        third = jnp.where(place == 0, down[2], jnp.where(place == 3, up[2], up[0]))
        top = jnp.maximum(jnp.maximum(top, first), jnp.maximum(second, third))
    return jnp.maximum(top, jnp.where(lane < 16, pltpu.roll(top, LANES - 16, 1), pltpu.roll(top, 16, 1)))


def place_in_cell(rep):
    rep = lax.rem(rep + 8, 64)
    y, z = rep // 16, lax.rem(rep // 4, 2)
    return lax.rem(rep // 8 + (y + 1) // 2, 2) * 4 + lax.rem(rep // 2, 2) * 2 + lax.rem(rep + z, 2)


def first_kernel(local_ref, base_ref, out_ref):
    rows = base_ref.shape[0] // UNIT
    ones = block_ones()
    lane = index_of((UNIT, LANES), 1) % QBLOCK
    mine = place_in_cell(lax.axis_index("rep"))
    base = base_ref[pl.ds(pl.multiple_of(mine * rows, UNIT), rows)]
    local = local_ref[...].astype(jnp.float32)
    starts = range(0, rows, UNIT)
    deltas = [base[i : i + UNIT] - local[j * rows + i : j * rows + i + UNIT] for j in range(UNIT) for i in starts]
    scales = []
    for first in range(0, len(deltas), QBLOCK):
        group = deltas[first : first + QBLOCK]
        scale = scale_of(packed_top(group, lane))
        scales += [jnp.where(lane == place_of(j), scale, 0.0) for j in range(len(group))]
    total = jnp.zeros((rows, LANES), jnp.float32)
    count = len(starts)
    scale = spread(jnp.concatenate(scales, axis=0), ones)
    value = code_of(jnp.concatenate(deltas, axis=0), scale) * scale
    total = value[:rows]
    for j in range(1, UNIT):
        total += value[j * rows : (j + 1) * rows]
    total = to_root(total, SUM_FACTOR)
    for j in range(UNIT):
        out_ref[j * rows : (j + 1) * rows] = total


def second_kernel(in_ref, out_ref, *, replicas):
    rows = in_ref.shape[0] // UNIT
    total = from_root(in_ref[:rows], SUM_FACTOR)
    for j in range(1, UNIT):
        total += from_root(in_ref[j * rows : (j + 1) * rows], SUM_FACTOR)
    average = total * (1.0 / replicas)
    scale = scale_of(full_top(average, index_of(average.shape, 1) % QBLOCK))
    message = to_root(code_of(average, scale) * scale, GRAD_FACTOR)
    for j in range(UNIT):
        out_ref[j * rows : (j + 1) * rows] = message


def third_kernel(in_ref, squares_ref):
    grad = from_root(in_ref[...], GRAD_FACTOR)
    total = jnp.sum((grad * grad).reshape(-1, UNIT, LANES), axis=0)
    squares_ref[...] = jnp.broadcast_to(jnp.sum(total, axis=0, keepdims=True), (UNIT, LANES))


def fourth_kernel(parts_ref, base_ref, momentum_ref, squares_ref, new_base_ref, new_momentum_ref, *, limit):
    squares = jnp.sum(jnp.sum(squares_ref[...], axis=0, keepdims=True), axis=1, keepdims=True)
    factor = limit / jnp.maximum(jnp.sqrt(squares), limit)
    scaled = factor * from_root(parts_ref[...], GRAD_FACTOR)
    momentum = decay * momentum_ref[...] + scaled
    new_momentum_ref[...] = momentum
    new_base_ref[...] = base_ref[...] - outer_rate * (scaled + decay * momentum)


def to_units(array):
    rows, width = array.shape
    return array.reshape(rows, width // LANES, LANES).transpose(1, 0, 2).reshape(rows * width // LANES, LANES)


def from_units(array, rows, width):
    return array.reshape(width // LANES, rows, LANES).transpose(1, 0, 2).reshape(rows, width)


def call(kernel, name, out_shape, *operands):
    return pl.pallas_call(kernel, name=name, compiler_params=PARAMS, out_shape=out_shape)(*operands)


def per_device(groups, local_params, base, momentum):
    replicas = lax.axis_size("rep")
    shards = lax.axis_size("fsdp")
    rows, width = base.shape
    units = rows * width // LANES
    cells, across = cell_groups()

    def exchange(array, peers):
        return lax.all_to_all(array, "rep", split_axis=0, concat_axis=0, tiled=True, axis_index_groups=peers)

    def exchange_roots(array, peers):
        array = exchange(array.astype(SENT).reshape(UNIT, units // UNIT, LANES), peers)
        return array.reshape(units, LANES).astype(jnp.float32)

    def shape(count):
        return jax.ShapeDtypeStruct((count, LANES), jnp.float32)

    base_units = to_units(base)
    local = local_params[0].reshape(rows, width // LANES, LANES).transpose(1, 0, 2)
    local = exchange(local, cells).reshape(units, LANES)
    sums = call(first_kernel, "quantize_and_add", shape(units), local, base_units)
    sums = exchange_roots(sums, across)
    parts = call(lambda *refs: second_kernel(*refs, replicas=replicas), "average_and_quantize", shape(units), sums)
    parts = exchange_roots(parts, cells)
    squares = call(third_kernel, "add_squares", shape(shards), parts)
    squares = lax.all_to_all(
        squares.reshape(shards, 1, LANES), ("rep", "fsdp"), split_axis=0, concat_axis=0, tiled=True, axis_index_groups=groups
    ).reshape(shards, LANES)
    limit = clip_ratio * float(rows * width * shards) ** 0.5
    new_base, new_momentum = call(
        lambda *refs: fourth_kernel(*refs, limit=limit),
        "update",
        (shape(units), shape(units)),
        parts,
        base_units,
        to_units(momentum),
        squares,
    )
    return from_units(new_base, rows, width), from_units(new_momentum, rows, width)


def cell_groups():
    cells = [
        [((2 * y + (a + (y + 1) // 2) % 2 + 7) % 8 * 4 + 2 * z + b) * 2 + (core + z) % 2 for a in range(2) for b in range(2) for core in range(2)]
        for y in range(4)
        for z in range(2)
    ]
    return cells, [list(group) for group in zip(*cells)]


def near_groups(mesh):
    replicas, shards = mesh.shape["rep"], mesh.shape["fsdp"]

    def index(y, z, core, x):
        return ((y * 4 + z % 4) * 2 + core) * shards + x * 2 + z // 4

    partner = {0: 6, 1: 7, 2: 4, 3: 5}
    return [
        [index(y, z, core, x) for x in range(shards // 2) for z in (low, 7 - low if core else partner[low])]
        for y in range(replicas // 8)
        for low in range(4)
        for core in range(2)
    ]


def solution(mesh):
    groups = near_groups(mesh)
    return jax.shard_map(
        lambda *arrays: per_device(groups, *arrays),
        mesh=mesh,
        in_specs=(P("rep", "fsdp", None), P("fsdp", None), P("fsdp", None)),
        out_specs=(P("fsdp", None), P("fsdp", None)),
        check_vma=False,
    )
```

```python
import math

import jax
import jax.numpy as jnp
from jax import lax
from jax.experimental import pallas as pl
from jax.experimental.pallas import tpu as pltpu
from jax.sharding import PartitionSpec as P

QBLOCK = 32
LANES = 128
UNIT = 8
PARAMS = pltpu.CompilerParams(vmem_limit_bytes=4 << 20)

eps = 1e-06
clip_ratio = 0.2
outer_rate = 0.7
decay = 0.9

SENT = jnp.float16
SUM_FACTOR = 512.0
GRAD_FACTOR = 1024.0

STAIR = (6.57973575592041, -12.987854957580566, 12.20757007598877, -6.687924861907959, 2.368926763534546, -0.5121700763702393)


def staircase(values):
    near = jnp.round(values)
    rest = values - near
    square = rest * rest
    poly = jnp.full_like(square, STAIR[-1])
    for coefficient in STAIR[-2::-1]:
        poly = poly * square + coefficient
    return near + rest * square * poly


def rounded(values):
    return values.astype(jnp.bfloat16).astype(jnp.float32)


def scale_of(top):
    return rounded((top + eps) * (1.0 / 7.0))


def code_of(values, scale):
    return rounded(staircase(values * pl.reciprocal(scale)))


def to_root(values, factor):
    root = jnp.sqrt(jnp.abs(values)) * factor
    return jnp.where(values < 0.0, -root, root)


def from_root(root, factor):
    root = root * (1.0 / factor)
    return root * jnp.abs(root)


def index_of(shape, axis):
    return lax.broadcasted_iota(jnp.int32, shape, axis)


def block_ones():
    shape = (LANES, LANES)
    return jnp.where(index_of(shape, 0) // QBLOCK == index_of(shape, 1) // QBLOCK, 1.0, 0.0).astype(jnp.bfloat16)


def spread(values, ones):
    return jnp.dot(values.astype(jnp.bfloat16), ones, preferred_element_type=jnp.float32)


def merged_four(arrays, lane, unit):
    merged = None
    for k, array in enumerate(arrays):
        place = 3 - (k % 2 * 2 + k // 2)
        top = array
        for other in range(4):
            if other != place:
                top = jnp.maximum(top, pltpu.roll(array, (place - other) * unit % LANES, 1))
        merged = top if merged is None else jnp.where(lane // unit % 4 == place, top, merged)
    return merged


def packed_top(arrays, lane):
    arrays = [jnp.abs(array) for array in arrays]
    arrays += [jnp.zeros_like(arrays[0])] * (-len(arrays) % 8)
    half = QBLOCK // 2
    halves = []
    for one, two in zip(arrays[::2], arrays[1::2]):
        one = jnp.maximum(one, pltpu.roll(one, half, 1))
        two = jnp.maximum(two, pltpu.roll(two, LANES - half, 1))
        halves.append(jnp.where(lane >= half, one, two))
    arrays = [merged_four(halves[k : k + 4], lane, 4) for k in range(0, len(halves), 4)]
    arrays += [jnp.zeros_like(arrays[0])] * (4 - len(arrays))
    return merged_four(arrays, lane, 1)


def place_of(j):
    return sum((QBLOCK // 2) >> bit for bit in range(5) if not (j >> bit) & 1)


def full_top(values, lane):
    top = jnp.abs(values)
    for shift in (1, 4):
        down = [pltpu.roll(top, LANES - shift * k, 1) for k in (1, 2, 3)]
        up = [pltpu.roll(top, shift * k, 1) for k in (1, 2, 3)]
        place = (lane // shift) % 4
        first = jnp.where(place < 3, down[0], up[0])
        second = jnp.where(place < 2, down[1], up[1])
        third = jnp.where(place == 0, down[2], jnp.where(place == 3, up[2], up[0]))
        top = jnp.maximum(jnp.maximum(top, first), jnp.maximum(second, third))
    return jnp.maximum(top, jnp.where(lane < 16, pltpu.roll(top, LANES - 16, 1), pltpu.roll(top, 16, 1)))


def place_in_cell(rep):
    rep = lax.rem(rep + 8, 64)
    y, z = rep // 16, lax.rem(rep // 4, 2)
    return lax.rem(rep // 8 + (y + 1) // 2, 2) * 4 + lax.rem(rep // 2, 2) * 2 + lax.rem(rep + z, 2)


def first_kernel(local_ref, base_ref, out_ref):
    rows = base_ref.shape[0] // UNIT
    ones = block_ones()
    lane = index_of((UNIT, LANES), 1) % QBLOCK
    mine = place_in_cell(lax.axis_index("rep"))
    base = base_ref[pl.ds(pl.multiple_of(mine * rows, UNIT), rows)]
    local = local_ref[...].astype(jnp.float32)
    starts = range(0, rows, UNIT)
    deltas = [base[i : i + UNIT] - local[j * rows + i : j * rows + i + UNIT] for j in range(UNIT) for i in starts]
    scales = []
    for first in range(0, len(deltas), QBLOCK):
        group = deltas[first : first + QBLOCK]
        scale = scale_of(packed_top(group, lane))
        scales += [jnp.where(lane == place_of(j), scale, 0.0) for j in range(len(group))]
    total = jnp.zeros((rows, LANES), jnp.float32)
    count = len(starts)
    scale = spread(jnp.concatenate(scales, axis=0), ones)
    value = code_of(jnp.concatenate(deltas, axis=0), scale) * scale
    total = value[:rows]
    for j in range(1, UNIT):
        total += value[j * rows : (j + 1) * rows]
    total = to_root(total, SUM_FACTOR)
    for j in range(UNIT):
        out_ref[j * rows : (j + 1) * rows] = total


def second_kernel(in_ref, out_ref, *, replicas):
    rows = in_ref.shape[0] // UNIT
    total = from_root(in_ref[:rows], SUM_FACTOR)
    for j in range(1, UNIT):
        total += from_root(in_ref[j * rows : (j + 1) * rows], SUM_FACTOR)
    average = total * (1.0 / replicas)
    scale = scale_of(full_top(average, index_of(average.shape, 1) % QBLOCK))
    message = to_root(code_of(average, scale) * scale, GRAD_FACTOR)
    for j in range(UNIT):
        out_ref[j * rows : (j + 1) * rows] = message


def third_kernel(in_ref, squares_ref):
    grad = from_root(in_ref[...], GRAD_FACTOR)
    total = jnp.sum((grad * grad).reshape(-1, UNIT, LANES), axis=0)
    squares_ref[...] = jnp.broadcast_to(jnp.sum(total, axis=0, keepdims=True), (UNIT, LANES))


def fourth_kernel(parts_ref, base_ref, momentum_ref, squares_ref, new_base_ref, new_momentum_ref, *, limit):
    squares = jnp.sum(jnp.sum(squares_ref[...], axis=0, keepdims=True), axis=1, keepdims=True)
    factor = limit / jnp.maximum(jnp.sqrt(squares), limit)
    scaled = factor * from_root(parts_ref[...], GRAD_FACTOR)
    momentum = decay * momentum_ref[...] + scaled
    new_momentum_ref[...] = momentum
    new_base_ref[...] = base_ref[...] - outer_rate * (scaled + decay * momentum)


def to_units(array):
    rows, width = array.shape
    return array.reshape(rows, width // LANES, LANES).transpose(1, 0, 2).reshape(rows * width // LANES, LANES)


def from_units(array, rows, width):
    return array.reshape(width // LANES, rows, LANES).transpose(1, 0, 2).reshape(rows, width)


def call(kernel, name, out_shape, *operands):
    return pl.pallas_call(kernel, name=name, compiler_params=PARAMS, out_shape=out_shape)(*operands)


def per_device(groups, local_params, base, momentum):
    replicas = lax.axis_size("rep")
    shards = lax.axis_size("fsdp")
    rows, width = base.shape
    units = rows * width // LANES
    cells, across = cell_groups()

    def exchange(array, peers):
        return lax.all_to_all(array, "rep", split_axis=0, concat_axis=0, tiled=True, axis_index_groups=peers)

    def exchange_roots(array, peers):
        array = exchange(array.astype(SENT).reshape(UNIT, units // UNIT, LANES), peers)
        return array.reshape(units, LANES).astype(jnp.float32)

    def shape(count):
        return jax.ShapeDtypeStruct((count, LANES), jnp.float32)

    base_units = to_units(base)
    local = local_params[0].reshape(rows, width // LANES, LANES).transpose(1, 0, 2)
    local = exchange(local, cells).reshape(units, LANES)
    sums = call(first_kernel, "quantize_and_add", shape(units), local, base_units)
    sums = exchange_roots(sums, across)
    parts = call(lambda *refs: second_kernel(*refs, replicas=replicas), "average_and_quantize", shape(units), sums)
    parts = exchange_roots(parts, cells)
    squares = call(third_kernel, "add_squares", shape(shards), parts)
    squares = lax.all_to_all(
        squares.reshape(shards, 1, LANES), ("rep", "fsdp"), split_axis=0, concat_axis=0, tiled=True, axis_index_groups=groups
    ).reshape(shards, LANES)
    limit = clip_ratio * float(rows * width * shards) ** 0.5
    new_base, new_momentum = call(
        lambda *refs: fourth_kernel(*refs, limit=limit),
        "update",
        (shape(units), shape(units)),
        parts,
        base_units,
        to_units(momentum),
        squares,
    )
    return from_units(new_base, rows, width), from_units(new_momentum, rows, width)


def cell_groups():
    cells = [
        [((2 * y + (a + (y + 1) // 2) % 2 + 7) % 8 * 4 + 2 * z + b) * 2 + (core + z) % 2 for a in range(2) for b in range(2) for core in range(2)]
        for y in range(4)
        for z in range(2)
    ]
    order = sorted(range(8), key=lambda k: (k // 2 != 2, k % 2 == 0, k))
    return cells, [[group[k] for k in order] for group in zip(*cells)]


def near_groups(mesh):
    replicas, shards = mesh.shape["rep"], mesh.shape["fsdp"]

    def index(y, z, core, x):
        return ((y * 4 + z % 4) * 2 + core) * shards + x * 2 + z // 4

    partner = {0: 6, 1: 7, 2: 4, 3: 5}
    return [
        [index(y, z, core, x) for x in range(shards // 2) for z in (low, 7 - low if core else partner[low])][::-1]
        for y in range(replicas // 8)
        for low in range(4)
        for core in range(2)
    ]


def solution(mesh):
    groups = near_groups(mesh)
    return jax.shard_map(
        lambda *arrays: per_device(groups, *arrays),
        mesh=mesh,
        in_specs=(P("rep", "fsdp", None), P("fsdp", None), P("fsdp", None)),
        out_specs=(P("fsdp", None), P("fsdp", None)),
        check_vma=False,
    )
```

```python
import math

import jax
import jax.numpy as jnp
from jax import lax
from jax.experimental import pallas as pl
from jax.experimental.pallas import tpu as pltpu
from jax.sharding import PartitionSpec as P

QBLOCK = 32
LANES = 128
UNIT = 8
PARAMS = pltpu.CompilerParams(vmem_limit_bytes=4 << 20)

eps = 1e-06
clip_ratio = 0.2
outer_rate = 0.7
decay = 0.9

SENT = jnp.float16
SUM_FACTOR = 512.0
GRAD_FACTOR = 1024.0

STAIR = (6.57973575592041, -12.987854957580566, 12.20757007598877, -6.687924861907959, 2.368926763534546, -0.5121700763702393)


def staircase(values):
    near = jnp.round(values)
    rest = values - near
    square = rest * rest
    poly = jnp.full_like(square, STAIR[-1])
    for coefficient in STAIR[-2::-1]:
        poly = poly * square + coefficient
    return near + rest * square * poly


def rounded(values):
    return values.astype(jnp.bfloat16).astype(jnp.float32)


def scale_of(top):
    return rounded((top + eps) * (1.0 / 7.0))


def code_of(values, scale):
    return rounded(staircase(values * pl.reciprocal(scale)))


def to_root(values, factor):
    root = jnp.sqrt(jnp.abs(values)) * factor
    return jnp.where(values < 0.0, -root, root)


def from_root(root, factor):
    root = root * (1.0 / factor)
    return root * jnp.abs(root)


def index_of(shape, axis):
    return lax.broadcasted_iota(jnp.int32, shape, axis)


def block_ones():
    shape = (LANES, LANES)
    return jnp.where(index_of(shape, 0) // QBLOCK == index_of(shape, 1) // QBLOCK, 1.0, 0.0).astype(jnp.bfloat16)


def spread(values, ones):
    return jnp.dot(values.astype(jnp.bfloat16), ones, preferred_element_type=jnp.float32)


def merged_four(arrays, lane, unit):
    merged = None
    for k, array in enumerate(arrays):
        place = 3 - (k % 2 * 2 + k // 2)
        top = array
        for other in range(4):
            if other != place:
                top = jnp.maximum(top, pltpu.roll(array, (place - other) * unit % LANES, 1))
        merged = top if merged is None else jnp.where(lane // unit % 4 == place, top, merged)
    return merged


def packed_top(arrays, lane):
    arrays = [jnp.abs(array) for array in arrays]
    arrays += [jnp.zeros_like(arrays[0])] * (-len(arrays) % 8)
    half = QBLOCK // 2
    halves = []
    for one, two in zip(arrays[::2], arrays[1::2]):
        one = jnp.maximum(one, pltpu.roll(one, half, 1))
        two = jnp.maximum(two, pltpu.roll(two, LANES - half, 1))
        halves.append(jnp.where(lane >= half, one, two))
    arrays = [merged_four(halves[k : k + 4], lane, 4) for k in range(0, len(halves), 4)]
    arrays += [jnp.zeros_like(arrays[0])] * (4 - len(arrays))
    return merged_four(arrays, lane, 1)


def place_of(j):
    return sum((QBLOCK // 2) >> bit for bit in range(5) if not (j >> bit) & 1)


def full_top(values, lane):
    top = jnp.abs(values)
    for shift in (1, 4):
        down = [pltpu.roll(top, LANES - shift * k, 1) for k in (1, 2, 3)]
        up = [pltpu.roll(top, shift * k, 1) for k in (1, 2, 3)]
        place = (lane // shift) % 4
        first = jnp.where(place < 3, down[0], up[0])
        second = jnp.where(place < 2, down[1], up[1])
        third = jnp.where(place == 0, down[2], jnp.where(place == 3, up[2], up[0]))
        top = jnp.maximum(jnp.maximum(top, first), jnp.maximum(second, third))
    return jnp.maximum(top, jnp.where(lane < 16, pltpu.roll(top, LANES - 16, 1), pltpu.roll(top, 16, 1)))


def place_in_cell(rep):
    rep = lax.rem(rep + 8, 64)
    y, z = rep // 16, lax.rem(rep // 4, 2)
    return lax.rem(rep // 8 + (y + 1) // 2, 2) * 4 + lax.rem(rep // 2, 2) * 2 + lax.rem(rep + z, 2)


def first_kernel(local_ref, base_ref, out_ref):
    rows = base_ref.shape[0] // UNIT
    ones = block_ones()
    lane = index_of((UNIT, LANES), 1) % QBLOCK
    mine = place_in_cell(lax.axis_index("rep"))
    base = base_ref[pl.ds(pl.multiple_of(mine * rows, UNIT), rows)]
    local = local_ref[...].astype(jnp.float32)
    starts = range(0, rows, UNIT)
    deltas = [base[i : i + UNIT] - local[j * rows + i : j * rows + i + UNIT] for j in range(UNIT) for i in starts]
    scales = []
    for first in range(0, len(deltas), QBLOCK):
        group = deltas[first : first + QBLOCK]
        scale = scale_of(packed_top(group, lane))
        scales += [jnp.where(lane == place_of(j), scale, 0.0) for j in range(len(group))]
    total = jnp.zeros((rows, LANES), jnp.float32)
    count = len(starts)
    scale = spread(jnp.concatenate(scales, axis=0), ones)
    value = code_of(jnp.concatenate(deltas, axis=0), scale) * scale
    total = value[:rows]
    for j in range(1, UNIT):
        total += value[j * rows : (j + 1) * rows]
    total = to_root(total, SUM_FACTOR)
    for j in range(UNIT):
        out_ref[j * rows : (j + 1) * rows] = total


def second_kernel(in_ref, out_ref, *, replicas):
    rows = in_ref.shape[0] // UNIT
    total = from_root(in_ref[:rows], SUM_FACTOR)
    for j in range(1, UNIT):
        total += from_root(in_ref[j * rows : (j + 1) * rows], SUM_FACTOR)
    average = total * (1.0 / replicas)
    scale = scale_of(full_top(average, index_of(average.shape, 1) % QBLOCK))
    message = to_root(code_of(average, scale) * scale, GRAD_FACTOR)
    for j in range(UNIT):
        out_ref[j * rows : (j + 1) * rows] = message


def third_kernel(in_ref, squares_ref):
    grad = from_root(in_ref[...], GRAD_FACTOR)
    total = jnp.sum((grad * grad).reshape(-1, UNIT, LANES), axis=0)
    squares_ref[...] = jnp.broadcast_to(jnp.sum(total, axis=0, keepdims=True), (UNIT, LANES))


def fourth_kernel(parts_ref, base_ref, momentum_ref, squares_ref, new_base_ref, new_momentum_ref, *, limit):
    squares = jnp.sum(jnp.sum(squares_ref[...], axis=0, keepdims=True), axis=1, keepdims=True)
    factor = limit / jnp.maximum(jnp.sqrt(squares), limit)
    scaled = factor * from_root(parts_ref[...], GRAD_FACTOR)
    momentum = decay * momentum_ref[...] + scaled
    new_momentum_ref[...] = momentum
    new_base_ref[...] = base_ref[...] - outer_rate * (scaled + decay * momentum)


def to_units(array):
    rows, width = array.shape
    return array.reshape(rows, width // LANES, LANES).transpose(1, 0, 2).reshape(rows * width // LANES, LANES)


def from_units(array, rows, width):
    return array.reshape(width // LANES, rows, LANES).transpose(1, 0, 2).reshape(rows, width)


def call(kernel, name, out_shape, *operands):
    return pl.pallas_call(kernel, name=name, compiler_params=PARAMS, out_shape=out_shape)(*operands)


def per_device(groups, local_params, base, momentum):
    replicas = lax.axis_size("rep")
    shards = lax.axis_size("fsdp")
    rows, width = base.shape
    units = rows * width // LANES
    cells, across = cell_groups()

    def exchange(array, peers):
        return lax.all_to_all(array, "rep", split_axis=0, concat_axis=0, tiled=True, axis_index_groups=peers)

    def exchange_roots(array, peers):
        array = exchange(array.astype(SENT).reshape(UNIT, units // UNIT, LANES), peers)
        return array.reshape(units, LANES).astype(jnp.float32)

    def shape(count):
        return jax.ShapeDtypeStruct((count, LANES), jnp.float32)

    base_units = to_units(base)
    local = local_params[0].reshape(rows, width // LANES, LANES).transpose(1, 0, 2)
    local = exchange(local, cells).reshape(units, LANES)
    sums = call(first_kernel, "quantize_and_add", shape(units), local, base_units)
    sums = exchange_roots(sums, across)
    parts = call(lambda *refs: second_kernel(*refs, replicas=replicas), "average_and_quantize", shape(units), sums)
    parts = exchange_roots(parts, cells)
    squares = call(third_kernel, "add_squares", shape(shards), parts)
    squares = lax.all_to_all(
        squares.reshape(shards, 1, LANES), ("rep", "fsdp"), split_axis=0, concat_axis=0, tiled=True, axis_index_groups=groups
    ).reshape(shards, LANES)
    limit = clip_ratio * float(rows * width * shards) ** 0.5
    new_base, new_momentum = call(
        lambda *refs: fourth_kernel(*refs, limit=limit),
        "update",
        (shape(units), shape(units)),
        parts,
        base_units,
        to_units(momentum),
        squares,
    )
    return from_units(new_base, rows, width), from_units(new_momentum, rows, width)


def cell_groups():
    cells = [
        [((2 * y + (a + (y + 1) // 2) % 2 + 7) % 8 * 4 + 2 * z + b) * 2 + (core + z) % 2 for a in range(2) for b in range(2) for core in range(2)]
        for y in range(4)
        for z in range(2)
    ]
    order = sorted(range(8), key=lambda k: (k // 2 != 2, k % 2 == 0, k))
    return cells, [[group[k] for k in order] for group in zip(*cells)]


def near_groups(mesh):
    replicas, shards = mesh.shape["rep"], mesh.shape["fsdp"]

    def index(y, z, core, x):
        return ((y * 4 + z % 4) * 2 + core) * shards + x * 2 + z // 4

    partner = {0: 6, 1: 7, 2: 4, 3: 5}
    return [
        [index(y, z, core, x) for z in (low, 7 - low if core else partner[low]) for x in range(shards // 2)][::-1]
        for y in range(replicas // 8)
        for low in range(4)
        for core in range(2)
    ]


def solution(mesh):
    groups = near_groups(mesh)
    return jax.shard_map(
        lambda *arrays: per_device(groups, *arrays),
        mesh=mesh,
        in_specs=(P("rep", "fsdp", None), P("fsdp", None), P("fsdp", None)),
        out_specs=(P("fsdp", None), P("fsdp", None)),
        check_vma=False,
    )
```
